256 devices in a mesh: chan: 16 (over x, z_hi, core), batch: 16 (over y, z_lo).
Axes of the slice: x: 4, y: 4, z: 8 (z_hi: 2, z_lo: 4; z = z_hi * 4 + z_lo), core: 2. Of those that a mesh axis runs over, the one named last changes fastest.
Arguments:
- fields: bfloat16 [16, 1536, 4096], P('batch', None, 'chan'), may hold values from -6 to 6
- norm1_gain: float32 [1536], replicated, may hold values from 0.5 to 1.5
- norm1_shift: float32 [1536], replicated, may hold values from -1.75 to 1.75
- spec_w1: float32 [2, 32, 48, 48], P(None, 'chan'), may hold values from -0.625 to 0.625
- spec_b1: float32 [2, 32, 48], P(None, 'chan'), may hold values from -1.75 to 1.75
- spec_w2: float32 [2, 32, 48, 48], P(None, 'chan'), may hold values from -0.625 to 0.625
- spec_b2: float32 [2, 32, 48], P(None, 'chan'), may hold values from -1.75 to 1.75
- norm2_gain: float32 [1536], replicated, may hold values from 0.5 to 1.5
- norm2_shift: float32 [1536], replicated, may hold values from -1.75 to 1.75
- w_in: bfloat16 [1536, 3072], P(None, 'batch'), may hold values from -0.15625 to 0.15625
- b_in: float32 [3072], replicated, may hold values from -1.75 to 1.75
- w_out: bfloat16 [3072, 1536], P('batch'), may hold values from -0.109375 to 0.109375
- b_out: float32 [1536], replicated, may hold values from -1.75 to 1.75
Outputs:
- mixed: bfloat16 [16, 1536, 4096], P('batch', None, 'chan')
The draws below stay inside these ranges and needn't reach their ends.
All inputs are finite; a program needn't handle non-finite values.
Results may differ from the reference program's by a relative error of at most 0.008.
Values may be sent and summed in bfloat16 or wider, within the bound.
A program may use at most 128 MiB of HBM per device.

```python
import jax
import jax.numpy as jnp
from jax import lax

D = 1536
BLOCKS = 32
BSIZE = 48
FF = 3072
GRID = 16
TOKENS = 4096
FRAMES = 16


def steps_of(own_key, dims, shards, least, top_value):
    level, own = 1.0, jax.random.fold_in(own_key, 6)
    for axis_at, parts in shards:
        draws = jnp.exp(jax.random.uniform(jax.random.fold_in(own, axis_at), (parts,), jnp.float32, least / len(shards), top_value / len(shards)))
        level = level * jnp.repeat(draws, dims[axis_at] // parts).reshape([-1 if axis == axis_at else 1 for axis in range(len(dims))])
    return level


def centred(own_key, dims, scale, limit, shards=(), dtype=jnp.bfloat16):
    drawn = jax.random.normal(own_key, dims, jnp.float32) * scale
    if len(shards) > 0:
        drawn = steps_of(own_key, dims, shards, -0.22, 0.18) * drawn
    return jnp.clip(drawn, min=-limit, max=limit).astype(dtype)


def setup_inputs(seed: int = 0) -> dict:
    keys = jax.random.split(jax.random.key(seed), 14)
    return {
        "fields": centred(keys[0], (FRAMES, D, TOKENS), 1.0, 6.0, ((0, 16), (2, 16))),
        "norm1_gain": jnp.clip(1.0 + 0.1 * jax.random.normal(keys[1], (D,), jnp.float32), 0.5, 1.5),
        "norm1_shift": centred(keys[2], (D,), 0.3, 1.75, (), jnp.float32),
        "spec_w1": centred(keys[3], (2, BLOCKS, BSIZE, BSIZE), (2 * BSIZE) ** -0.5, 0.625, ((1, 16),), jnp.float32),
        "spec_b1": centred(keys[4], (2, BLOCKS, BSIZE), 0.3, 1.75, ((1, 16),), jnp.float32),
        "spec_w2": centred(keys[5], (2, BLOCKS, BSIZE, BSIZE), (2 * BSIZE) ** -0.5, 0.625, ((1, 16),), jnp.float32),
        "spec_b2": centred(keys[6], (2, BLOCKS, BSIZE), 0.3, 1.75, ((1, 16),), jnp.float32),
        "norm2_gain": jnp.clip(1.0 + 0.1 * jax.random.normal(keys[7], (D,), jnp.float32), 0.5, 1.5),
        "norm2_shift": centred(keys[8], (D,), 0.3, 1.75, (), jnp.float32),
        "w_in": centred(keys[9], (D, FF), D ** -0.5, 0.15625, ((1, 16),)),
        "b_in": centred(keys[10], (FF,), 0.3, 1.75, (), jnp.float32),
        "w_out": centred(keys[11], (FF, D), FF ** -0.5, 0.109375, ((0, 16),)),
        "b_out": centred(keys[12], (D,), 0.3, 1.75, (), jnp.float32),
    }


highest = lax.Precision.HIGHEST
shrink_level = 0.2

def layer_norm(values, gain_vec, shift_vec):
    widened = values.astype(jnp.float32)
    center = widened - lax.optimization_barrier(jnp.mean(widened, axis=0, keepdims=True))
    spread = lax.optimization_barrier(jnp.mean(center * center, axis=0, keepdims=True))
    return center * lax.rsqrt(spread + 1e-05) * gain_vec[:, None] + shift_vec[:, None]

def block_mix(values, weight):
    return jnp.einsum('bixyz,bio->boxyz', values, weight, precision=highest)

def with_bias(bias_vec):
    return bias_vec[:, :, None, None, None]

def shrink(values):
    return jnp.where(values > shrink_level, values - shrink_level, jnp.where(values < -shrink_level, values + shrink_level, jnp.zeros_like(values)))

def reference(fields, norm1_gain, norm1_shift, spec_w1, spec_b1, spec_w2, spec_b2, norm2_gain, norm2_shift, w_in, b_in, w_out, b_out):
    w_in_wide = w_in.astype(jnp.float32)
    w_out_wide = w_out.astype(jnp.float32)

    def one_frame(frame):
        normed = layer_norm(frame, norm1_gain, norm1_shift).astype(jnp.bfloat16)
        volume = normed.astype(jnp.float32).reshape(D, GRID, GRID, GRID)
        spectrum = jnp.fft.rfftn(volume, axes=(1, 2, 3), norm='ortho')
        half_count = GRID // 2 + 1
        spec_re = jnp.real(spectrum).reshape(BLOCKS, BSIZE, GRID, GRID, half_count)
        spec_im = jnp.imag(spectrum).reshape(BLOCKS, BSIZE, GRID, GRID, half_count)
        mid_re = jax.nn.gelu(block_mix(spec_re, spec_w1[0]) - block_mix(spec_im, spec_w1[1]) + with_bias(spec_b1[0]), approximate=False)
        mid_im = jax.nn.gelu(block_mix(spec_im, spec_w1[0]) + block_mix(spec_re, spec_w1[1]) + with_bias(spec_b1[1]), approximate=False)
        out_re = shrink(block_mix(mid_re, spec_w2[0]) - block_mix(mid_im, spec_w2[1]) + with_bias(spec_b2[0]))
        out_im = shrink(block_mix(mid_im, spec_w2[0]) + block_mix(mid_re, spec_w2[1]) + with_bias(spec_b2[1]))
        joined = lax.complex(out_re, out_im).reshape(D, GRID, GRID, half_count)
        spatial = jnp.fft.irfftn(joined, s=(GRID, GRID, GRID), axes=(1, 2, 3), norm='ortho')
        filtered = (spatial.reshape(D, TOKENS) + normed.astype(jnp.float32)).astype(jnp.bfloat16)
        hidden_state = frame.astype(jnp.float32) + filtered.astype(jnp.float32)
        z_norm = layer_norm(hidden_state, norm2_gain, norm2_shift).astype(jnp.bfloat16)
        z_rows = jnp.transpose(z_norm.astype(jnp.float32))
        pre_act = jnp.dot(z_rows, w_in_wide, precision=highest) + b_in
        units = jax.nn.gelu(pre_act, approximate=False).astype(jnp.bfloat16)
        projected = jnp.dot(units.astype(jnp.float32), w_out_wide, precision=highest)
        return (hidden_state + jnp.transpose(projected) + b_out[:, None]).astype(jnp.bfloat16)
    return lax.map(one_frame, fields)
```

```python
import math

import jax
import jax.numpy as jnp
import numpy as np
from jax import lax
from jax.experimental import pallas as pl
from jax.experimental.pallas import tpu as pltpu
from jax.sharding import PartitionSpec as P

D = 1536
TOK = 256
CH = 96
HALF = 48
GRID = 16
MODES = 144
SHRINK = 0.2
MESH = pl.DeviceIdType.MESH
F32 = jnp.float32
BF16 = jnp.bfloat16


def plane_tables():
    pos = np.arange(GRID)
    freq = np.arange(GRID // 2 + 1)
    phase = (
        pos[:, None, None, None] * pos[None, None, :, None]
        + pos[None, :, None, None] * freq[None, None, None, :]
    ) % GRID
    angle = phase * (2.0 * math.pi / GRID)
    cos = np.cos(angle).reshape(TOK, MODES) / 64.0
    sin = np.sin(angle).reshape(TOK, MODES) / 64.0
    weight = np.tile(np.where((freq == 0) | (freq == GRID // 2), 1.0, 2.0), GRID)
    forward = np.concatenate([cos, -sin], axis=1).T
    inverse = np.zeros((512, TOK))
    inverse[:MODES] = (cos * weight).T
    inverse[256 : 256 + MODES] = -(sin * weight).T
    return jnp.asarray(forward, BF16), jnp.asarray(inverse, BF16)


def turned(value, step, sign):
    re, im = value
    step = step % 16
    if step == 0:
        return value
    if step == 8:
        return (-re, -im)
    if step == 4:
        return (-im, re) if sign > 0 else (im, -re)
    if step == 12:
        return (im, -re) if sign > 0 else (-im, re)
    c = math.cos(2.0 * math.pi * step / 16)
    s = sign * math.sin(2.0 * math.pi * step / 16)
    return (re * c - im * s, re * s + im * c)


def fft_list(values, sign):
    n = len(values)
    if n == 1:
        return values
    even = fft_list(values[0::2], sign)
    odd = fft_list(values[1::2], sign)
    out = [None] * n
    for k in range(n // 2):
        t = turned(odd[k], k * (16 // n), sign)
        e = even[k]
        out[k] = (e[0] + t[0], e[1] + t[1])
        out[k + n // 2] = (e[0] - t[0], e[1] - t[1])
    return out


def erf(v):
    x = jnp.clip(v, -3.832506856900711, 3.832506856900711)
    s = x * x
    p = -2.72614225801306e-10 * s + 2.77068142495902e-08
    p = p * s - 2.10102402082508e-06
    p = p * s - 5.69250639462346e-05
    p = p * s - 7.34990630326855e-04
    p = p * s - 2.95459980854025e-03
    p = p * s - 1.60960333262415e-02
    q = -1.45660718464996e-05 * s - 2.13374055278905e-04
    q = q * s - 1.68282697438203e-03
    q = q * s - 7.37332916720468e-03
    q = q * s - 1.42647390514189e-02
    return x * p / q


def gelu(v):
    half = 0.5 * v
    return half + half * erf(v * 0.7071067811865476)


def shrink(v):
    return v - jnp.clip(v, -SHRINK, SHRINK)


def dot_nt(a, b):
    return lax.dot_general(a, b, (((1,), (1,)), ((), ())), preferred_element_type=F32)


def dot(a, b):
    return jnp.dot(a, b, preferred_element_type=F32)


def loop(n, body):
    def step(i, carry):
        body(i)
        return carry

    lax.fori_loop(0, n, step, 0)


def kernel(
    fields, vecs, b_in, win, wout, mix1, mix2, bias1, bias2, fwd, inv, out,
    normed, recv1, plane, mid, back, fil, recv2, hid, zt, act, part, precv, own_t,
    win_all, wout_all,
    s1, r1, s2, r2, loc, zs, zr, ps, pr,
    b1s, b1r, b2s, b2r, b3s, b3r, a1s, a1r, a2s, a2r, a3s, a3r, a4s, a4r,
):
    chan = lax.axis_index("chan")
    batch = lax.axis_index("batch")
    x, zh, core = chan // 4, (chan // 2) % 2, chan % 2
    y, zl = batch // 4, batch % 4
    z = zh * 4 + zl

    def dev(xx, yy, zz, cc):
        xx, yy, zz = xx % 4, yy % 4, zz % 8
        return ((xx * 2 + zz // 4) * 2 + cc, yy * 4 + zz % 4)

    def remote(src, dst, ss, rs, to):
        return pltpu.make_async_remote_copy(
            src_ref=src, dst_ref=dst, send_sem=ss, recv_sem=rs, device_id=to, device_id_type=MESH
        )

    def peer(j, way):
        dz, dx, dc = j // 8, (j // 2) % 4, j % 2
        px, pz, pc = (x + way * dx + 4) % 4, (zh + dz) % 2, (core + dc) % 2
        return (px * 2 + pz) * 2 + pc

    zp, zm = dev(x, y, z + 1, core), dev(x, y, z + 7, core)
    zp2, zm2 = dev(x, y, z + 2, core), dev(x, y, z + 6, core)
    yp, ym, y2 = dev(x, y + 1, z, core), dev(x, y + 3, z, core), dev(x, y + 2, z, core)
    xp, xm = dev(x + 1, y, z, core), dev(x + 3, y, z, core)
    mate = dev(x, y, z, 1 - core)

    barrier = pltpu.get_barrier_semaphore()

    def greet(j, carry):
        pl.semaphore_signal(barrier, inc=1, device_id=(peer(j, 1), batch), device_id_type=MESH)
        return carry

    lax.fori_loop(1, 16, greet, 0)
    for to in (zp, zm, zp2, zm2, yp, ym, y2):
        pl.semaphore_signal(barrier, inc=1, device_id=to, device_id_type=MESH)

    offs = (0, 3, 1, 2)

    def slot(dy, k):
        return ((y + dy) % 4) * 4 + (zl + offs[k]) % 4

    own_slot = slot(0, 0)
    keep_in = pltpu.make_async_copy(win, win_all.at[own_slot], loc.at[0])
    keep_in.start()
    keep_out = pltpu.make_async_copy(
        wout.at[:, pl.ds(pl.multiple_of(x * 384, 128), 384)], wout_all.at[x, own_slot], loc.at[1]
    )
    keep_out.start()

    def rows(i):
        return pl.ds(pl.multiple_of(i * CH, CH), CH)

    def norm(load, gain_at, write):
        def add(i, acc):
            return acc + jnp.sum(load(i).reshape(CH // 8, 8, TOK), axis=0)

        total = lax.fori_loop(0, 16, add, jnp.zeros((8, TOK), F32))
        mean = jnp.sum(total, axis=0, keepdims=True) * (1.0 / D)

        def add_square(i, acc):
            c = load(i) - mean
            return acc + jnp.sum((c * c).reshape(CH // 8, 8, TOK), axis=0)

        total = lax.fori_loop(0, 16, add_square, jnp.zeros((8, TOK), F32))
        var = jnp.sum(total, axis=0, keepdims=True) * (1.0 / D)
        scale = lax.rsqrt(var + 1e-05)

        def finish(i):
            v = vecs[rows(i), :]
            c = load(i) - mean
            gain, shift = v[:, gain_at : gain_at + 1], v[:, gain_at + 1 : gain_at + 2]
            write(i, (c * scale * gain + shift).astype(BF16))

        loop(16, finish)

    def load_fields(i):
        return fields[rows(i), :].astype(F32)

    def write_normed(i, v):
        normed[rows(i), :] = v

    norm(load_fields, 0, write_normed)
    pl.semaphore_wait(barrier, 22)

    def to_block(j):
        return remote(
            normed.at[rows(peer(j, 1))], recv1.at[chan, pl.ds(0, CH)], s1.at[j], r1.at[j], (peer(j, 1), batch)
        )

    def from_plane(j):
        return remote(
            normed.at[rows(chan)], recv1.at[peer(j, -1), pl.ds(0, CH)], s1.at[j], r1.at[j], (peer(j, 1), batch)
        )

    loop(15, lambda i: to_block(15 - i).start())
    keep = pltpu.make_async_copy(normed.at[rows(chan)], recv1.at[chan, pl.ds(0, CH)], loc.at[2])
    keep.start()

    def b2(k, way):
        at = win_all.at[slot(0, k)]
        return remote(at, at, b2s.at[way, k], b2r.at[way, k], ym if way else yp)

    def b2_in(k, way):
        at = win_all.at[slot(1 if way else 3, k)]
        return remote(at, at, b2s.at[way, k], b2r.at[way, k], ym if way else yp)

    def b3(k):
        at = win_all.at[slot(3 if k < 2 else 1, k)]
        return remote(at, at, b3s.at[k], b3r.at[k], yp if k < 2 else ym)

    def b3_in(k):
        at = win_all.at[slot(2, k)]
        return remote(at, at, b3s.at[k], b3r.at[k], yp if k < 2 else ym)

    keep_in.wait()
    keep_out.wait()
    b2(0, 0).start()
    b2(0, 1).start()

    def b1(k, half, frm):
        to = {1: zp, 2: zm, 3: zm2 if half else zp2}[k]
        span = pl.ds(0, CH) if k < 3 else pl.ds(half * HALF, HALF)
        n = k + half
        at = win_all.at[slot(0, k if frm else 0), span]
        return remote(at, at, b1s.at[n], b1r.at[n], to)

    def a1(k, frm):
        at = wout_all.at[x, slot(0, k if frm else 0)]
        to = {1: zp, 2: zm, 3: dev(x, y, z + 2 + 4 * core, core)}[k]
        return remote(at, at, a1s.at[k], a1r.at[k], to)

    for k in (1, 2, 3):
        a1(k, False).start()
    for k, half in ((1, 0), (2, 0), (3, 0), (3, 1)):
        b1(k, half, False).start()

    group_offs = (0, 3, 1, 2)

    def group(q, dy):
        return wout_all.at[q, pl.ds(((y + dy) % 4) * 4, 4)]

    def a2(r, frm):
        to = {1: yp, 2: ym, 3: y2}[r]
        at = group(x, group_offs[r] if frm else 0)
        return remote(at, at, a2s.at[r], a2r.at[r], to)

    def a3(r, way, frm):
        q = (x + ((1 if way else 3) if frm else 0)) % 4
        at = group(q, group_offs[r])
        return remote(at, at, a3s.at[way, r], a3r.at[way, r], xm if way else xp)

    def a4(r, frm):
        q = (x + (2 if frm else (3 if r < 2 else 1))) % 4
        at = group(q, group_offs[r])
        return remote(at, at, a4s.at[r], a4r.at[r], xp if r < 2 else xm)

    def service_z():
        for k in (1, 2, 3):
            a1(k, True).wait_recv()
        for r in (1, 2, 3):
            a2(r, False).start()
        a3(0, 0, False).start()
        a3(0, 1, False).start()
        for k in (1, 2, 3):
            b1(k, 0, True).wait_recv()
            if k == 3:
                b1(k, 1, True).wait_recv()
            b2(k, 0).start()
            b2(k, 1).start()

    def service_y():
        for k in (0, 1):
            b2_in(k, 0).wait_recv()
            b3(k).start()
        for k in (2, 3):
            b2_in(k, 1).wait_recv()
            b3(k).start()
        for r in (1, 2, 3):
            a2(r, True).wait_recv()
            a3(r, 0, False).start()
            a3(r, 1, False).start()

    def service_x():
        for r in (0, 1):
            a3(r, 0, True).wait_recv()
            a4(r, False).start()
        for r in (2, 3):
            a3(r, 1, True).wait_recv()
            a4(r, False).start()

    def clear(a):
        recv1[a, pl.ds(CH, 32), :] = jnp.zeros((32, TOK), BF16)
        back[a, :, pl.ds(128, 128)] = jnp.zeros((2 * CH, 128), F32)

    loop(16, clear)

    keep.wait()
    loop(15, lambda i: from_plane(15 - i).wait_recv())

    def planes(p):
        both = recv1[pl.ds(2 * p, 2)].reshape(256, TOK)
        plane[p] = dot_nt(fwd[...], both)

    loop(8, planes)
    service_z()

    def lines(t):
        re_at = pl.ds(pl.multiple_of(t * 8, 8), 8)
        im_at = pl.ds(pl.multiple_of(MODES + t * 8, 8), 8)
        vals = []
        for a in range(16):
            lanes = pl.ds((a % 2) * 128, 128)
            vals.append((plane[a // 2, re_at, lanes], plane[a // 2, im_at, lanes]))
        for a, (re, im) in enumerate(fft_list(vals, -1)):
            lanes = pl.ds((a % 2) * 128, 128)
            plane[a // 2, re_at, lanes] = re
            plane[a // 2, im_at, lanes] = im

    loop(18, lines)

    def mix(p):
        v = plane[p].astype(BF16)
        lhs = jnp.concatenate(
            [
                jnp.concatenate([v[:MODES, :128], v[MODES:, :128]], axis=1),
                jnp.concatenate([v[:MODES, 128:], v[MODES:, 128:]], axis=1),
            ],
            axis=0,
        )
        mid[...] = gelu(dot(lhs, mix1[...]) + bias1[...]).astype(BF16)
        for half in range(2):
            res = dot_nt(mix2[...], mid[pl.ds(half * MODES, MODES), :]) + bias2[...]
            back[2 * p + half, :, pl.ds(0, MODES)] = shrink(res)

    loop(8, mix)

    def lines_back(t):
        re_at = pl.ds(pl.multiple_of((t // 2) * 8, 8), 8)
        im_at = pl.ds(pl.multiple_of(CH + (t // 2) * 8, 8), 8)
        lanes = pl.ds(pl.multiple_of((t % 2) * 128, 128), 128)
        vals = [(back[a, re_at, lanes], back[a, im_at, lanes]) for a in range(16)]
        for a, (re, im) in enumerate(fft_list(vals, 1)):
            back[a, re_at, lanes] = re
            back[a, im_at, lanes] = im

    loop(24, lines_back)

    def planes_back(p):
        lhs = [
            jnp.concatenate([back[2 * p + i, :CH, :], back[2 * p + i, CH:, :]], axis=1).astype(BF16)
            for i in range(2)
        ]
        res = dot(jnp.concatenate(lhs, axis=0), inv[...])
        for i in range(2):
            v = res[i * CH : (i + 1) * CH] + recv1[2 * p + i, pl.ds(0, CH), :].astype(F32)
            fil[2 * p + i] = v.astype(BF16)

    loop(8, planes_back)

    def to_plane(j):
        return remote(fil.at[peer(j, 1)], recv2.at[rows(chan)], s2.at[j], r2.at[j], (peer(j, 1), batch))

    def from_block(j):
        return remote(fil.at[chan], recv2.at[rows(peer(j, -1))], s2.at[j], r2.at[j], (peer(j, 1), batch))

    loop(15, lambda i: to_plane(15 - i).start())
    keep = pltpu.make_async_copy(fil.at[chan], recv2.at[rows(chan)], loc.at[3])
    keep.start()
    service_y()
    service_x()
    keep.wait()
    loop(15, lambda i: from_block(15 - i).wait_recv())

    def hidden(i):
        hid[rows(i), :] = load_fields(i) + recv2[rows(i), :].astype(F32)

    loop(16, hidden)

    def write_z(i, v):
        recv2[rows(i), :] = v

    def load_hidden(i):
        return hid[rows(i), :]

    norm(load_hidden, 2, write_z)

    eye = (
        lax.broadcasted_iota(jnp.int32, (TOK, TOK), 0) == lax.broadcasted_iota(jnp.int32, (TOK, TOK), 1)
    ).astype(F32).astype(BF16)

    def turn(i):
        at = pl.ds(pl.multiple_of(i * 256, 256), 256)
        zt[0, :, at] = dot_nt(eye, recv2[at, :]).astype(BF16)

    loop(6, turn)
    send_z = remote(zt.at[0], zt.at[1], zs, zr, mate)
    send_z.start()

    def units(g, t):
        s0 = g * 4
        w = win_all[pl.ds(s0, 4)].reshape(384, D)
        at = pl.ds(pl.multiple_of(g * 384, 128), 384)
        act[t, :, at] = gelu(dot_nt(zt[t], w) + b_in[:, at]).astype(BF16)

    for k in (0, 1, 2, 3):
        for way in (0, 1):
            if (way == 0) != (k < 2):
                b2_in(k, way).wait_recv()
    for k in range(4):
        b3_in(k).wait_recv()
    loop(4, lambda g: units(g, 0))
    send_z.wait_recv()
    loop(4, lambda g: units(g, 1))

    for r in range(4):
        a3(r, 0 if r >= 2 else 1, True).wait_recv()
    for r in range(4):
        a4(r, True).wait_recv()

    def project_mate(q):
        at = pl.ds(pl.multiple_of(q * 384, 128), 384)
        part[:, at] = dot(act[1], wout_all[q].reshape(D, 384)).astype(BF16)

    loop(4, project_mate)
    send_part = remote(part, precv, ps, pr, mate)
    send_part.start()

    def project_own(q):
        at = pl.ds(pl.multiple_of(q * 384, 128), 384)
        own_t[:, at] = dot(act[0], wout_all[q].reshape(D, 384))

    loop(4, project_own)
    send_part.wait_recv()

    def finish(i):
        at = pl.ds(pl.multiple_of(i * 128, 128), 128)
        total = (own_t[:, at] + precv[:, at].astype(F32)).T
        out[at, :] = (hid[at, :] + total + vecs[at, :][:, 4:5]).astype(BF16)

    loop(12, finish)

    loop(15, lambda i: to_block(15 - i).wait_send())
    loop(15, lambda i: to_plane(15 - i).wait_send())
    send_z.wait_send()
    send_part.wait_send()
    for k, half in ((1, 0), (2, 0), (3, 0), (3, 1)):
        b1(k, half, False).wait_send()
    for k in (1, 2, 3):
        a1(k, False).wait_send()
        a2(k, False).wait_send()
    for k in range(4):
        for way in range(2):
            b2(k, way).wait_send()
            a3(k, way, False).wait_send()
        b3(k).wait_send()
        a4(k, False).wait_send()


def blocks_matrix(w, b):
    def diag(m):
        zero = jnp.zeros((HALF, HALF), F32)
        top = jnp.concatenate([m[0], zero], axis=1)
        low = jnp.concatenate([zero, m[1]], axis=1)
        return jnp.concatenate([top, low], axis=0)

    re, im = diag(w[0]), diag(w[1])
    full = jnp.stack([jnp.stack([re, im]), jnp.stack([-im, re])])
    return full, b.reshape(2, CH)


def on_device(
    fields, norm1_gain, norm1_shift, spec_w1, spec_b1, spec_w2, spec_b2,
    norm2_gain, norm2_shift, w_in, b_in, w_out, b_out,
):
    core = lax.axis_index("chan") % 2
    forward, inverse = plane_tables()
    m1, c1 = blocks_matrix(spec_w1, spec_b1)
    m1 = jnp.pad(m1, ((0, 0), (0, 0), (0, 32), (0, 32))).transpose(0, 2, 1, 3).reshape(256, 256)
    c1 = jnp.pad(c1, ((0, 0), (0, 32))).reshape(1, 256)
    m2, c2 = blocks_matrix(spec_w2, spec_b2)
    m2 = jnp.pad(m2, ((0, 0), (0, 0), (0, 32), (0, 0))).transpose(1, 3, 0, 2).reshape(192, 256)
    c2 = c2.reshape(192, 1)
    vecs = jnp.stack([norm1_gain, norm1_shift, norm2_gain, norm2_shift, b_out], axis=1)
    win = lax.dynamic_slice(w_in, (0, core * CH), (D, CH)).T
    wout = lax.dynamic_slice(w_out, (core * CH, 0), (CH, D))
    units_bias = lax.dynamic_slice(b_in.reshape(16, 2, CH), (0, core, 0), (16, 1, CH)).reshape(1, D)
    vmem = pl.BlockSpec(memory_space=pltpu.VMEM)
    dma = pltpu.SemaphoreType.DMA
    res = pl.pallas_call(
        kernel,
        out_shape=jax.ShapeDtypeStruct((D, TOK), BF16),
        in_specs=[vmem] * 11,
        out_specs=vmem,
        scratch_shapes=[
            pltpu.VMEM((D, TOK), BF16),
            pltpu.VMEM((16, 128, TOK), BF16),
            pltpu.VMEM((8, 2 * MODES, 256), F32),
            pltpu.VMEM((2 * MODES, 256), BF16),
            pltpu.VMEM((16, 2 * CH, 256), F32),
            pltpu.VMEM((16, CH, TOK), BF16),
            pltpu.VMEM((D, TOK), BF16),
            pltpu.VMEM((D, TOK), F32),
            pltpu.VMEM((2, TOK, D), BF16),
            pltpu.VMEM((2, TOK, D), BF16),
            pltpu.VMEM((TOK, D), BF16),
            pltpu.VMEM((TOK, D), BF16),
            pltpu.VMEM((TOK, D), F32),
            pltpu.VMEM((16, CH, D), BF16),
            pltpu.VMEM((4, 16, CH, 384), BF16),
            dma((16,)), dma((16,)), dma((16,)), dma((16,)), dma((4,)),
            dma, dma, dma, dma,
            dma((5,)), dma((5,)), dma((2, 4)), dma((2, 4)), dma((4,)), dma((4,)),
            dma((4,)), dma((4,)), dma((4,)), dma((4,)), dma((2, 4)), dma((2, 4)), dma((4,)), dma((4,)),
        ],
        compiler_params=pltpu.CompilerParams(
            collective_id=0, has_side_effects=True, vmem_limit_bytes=56 * 2**20
        ),
        name="block",
    )(
        fields[0], vecs, units_bias, win, wout, m1.astype(BF16), m2.astype(BF16), c1, c2, forward, inverse
    )
    return res[None]


def solution(mesh):
    return jax.shard_map(
        on_device,
        mesh=mesh,
        in_specs=(
            P("batch", None, "chan"),
            P(),
            P(),
            P(None, "chan", None, None),
            P(None, "chan", None),
            P(None, "chan", None, None),
            P(None, "chan", None),
            P(),
            P(),
            P(None, "batch"),
            P(),
            P("batch", None),
            P(),
        ),
        out_specs=P("batch", None, "chan"),
        check_vma=False,
    )
```

```python
import math

import jax
import jax.numpy as jnp
import numpy as np
from jax import lax
from jax.experimental import pallas as pl
from jax.experimental.pallas import tpu as pltpu
from jax.sharding import PartitionSpec as P

D = 1536
TOK = 256
CH = 96
HALF = 48
GRID = 16
MODES = 144
SHRINK = 0.2
MESH = pl.DeviceIdType.MESH
F32 = jnp.float32
BF16 = jnp.bfloat16


def plane_tables():
    pos = np.arange(GRID)
    freq = np.arange(GRID // 2 + 1)
    phase = (
        pos[:, None, None, None] * pos[None, None, :, None]
        + pos[None, :, None, None] * freq[None, None, None, :]
    ) % GRID
    angle = phase * (2.0 * math.pi / GRID)
    cos = np.cos(angle).reshape(TOK, MODES) / 64.0
    sin = np.sin(angle).reshape(TOK, MODES) / 64.0
    weight = np.tile(np.where((freq == 0) | (freq == GRID // 2), 1.0, 2.0), GRID)
    forward = np.concatenate([cos, -sin], axis=1).T
    inverse = np.zeros((512, TOK))
    inverse[:MODES] = (cos * weight).T
    inverse[256 : 256 + MODES] = -(sin * weight).T
    return jnp.asarray(forward, BF16), jnp.asarray(inverse, BF16)


def turned(value, step, sign):
    re, im = value
    step = step % 16
    if step == 0:
        return value
    if step == 8:
        return (-re, -im)
    if step == 4:
        return (-im, re) if sign > 0 else (im, -re)
    if step == 12:
        return (im, -re) if sign > 0 else (-im, re)
    c = math.cos(2.0 * math.pi * step / 16)
    s = sign * math.sin(2.0 * math.pi * step / 16)
    return (re * c - im * s, re * s + im * c)


def fft_list(values, sign):
    n = len(values)
    if n == 1:
        return values
    even = fft_list(values[0::2], sign)
    odd = fft_list(values[1::2], sign)
    out = [None] * n
    for k in range(n // 2):
        t = turned(odd[k], k * (16 // n), sign)
        e = even[k]
        out[k] = (e[0] + t[0], e[1] + t[1])
        out[k + n // 2] = (e[0] - t[0], e[1] - t[1])
    return out


def erf(v):
    x = jnp.clip(v, -3.832506856900711, 3.832506856900711)
    s = x * x
    p = -2.72614225801306e-10 * s + 2.77068142495902e-08
    p = p * s - 2.10102402082508e-06
    p = p * s - 5.69250639462346e-05
    p = p * s - 7.34990630326855e-04
    p = p * s - 2.95459980854025e-03
    p = p * s - 1.60960333262415e-02
    q = -1.45660718464996e-05 * s - 2.13374055278905e-04
    q = q * s - 1.68282697438203e-03
    q = q * s - 7.37332916720468e-03
    q = q * s - 1.42647390514189e-02
    return x * p / q


def gelu(v):
    half = 0.5 * v
    return half + half * erf(v * 0.7071067811865476)


def shrink(v):
    return v - jnp.clip(v, -SHRINK, SHRINK)


def dot_nt(a, b):
    return lax.dot_general(a, b, (((1,), (1,)), ((), ())), preferred_element_type=F32)


def dot(a, b):
    return jnp.dot(a, b, preferred_element_type=F32)


def loop(n, body):
    def step(i, carry):
        body(i)
        return carry

    lax.fori_loop(0, n, step, 0)


def kernel(
    fields, vecs, b_in, win, wout, mix1, mix2, bias1, bias2, fwd, inv, out,
    normed, recv1, plane, mid, back, fil, recv2, hid, zt, act, part, precv, own_t,
    w_all,
    s1, r1, s2, r2, loc, zs, zr, ps, pr,
    zws, zwr, xs, xr, ys, yr, y2s, y2r, ays, ayr, axs, axr, ax2s, ax2r,
):
    chan = lax.axis_index("chan")
    batch = lax.axis_index("batch")
    x, zh, core = chan // 4, (chan // 2) % 2, chan % 2
    y, zl = batch // 4, batch % 4
    z = zh * 4 + zl

    def dev(xx, yy, zz, cc):
        xx, yy, zz = xx % 4, yy % 4, zz % 8
        return ((xx * 2 + zz // 4) * 2 + cc, yy * 4 + zz % 4)

    def remote(src, dst, ss, rs, to):
        return pltpu.make_async_remote_copy(
            src_ref=src, dst_ref=dst, send_sem=ss, recv_sem=rs, device_id=to, device_id_type=MESH
        )

    def peer(j, way):
        dz, dx, dc = j // 8, (j // 2) % 4, j % 2
        px, pz, pc = (x + way * dx + 4) % 4, (zh + dz) % 2, (core + dc) % 2
        return (px * 2 + pz) * 2 + pc

    zp, zm = dev(x, y, z + 1, core), dev(x, y, z + 7, core)
    zp2, zm2 = dev(x, y, z + 2, core), dev(x, y, z + 6, core)
    yp, ym, y2 = dev(x, y + 1, z, core), dev(x, y + 3, z, core), dev(x, y + 2, z, core)
    xp, xm, x2 = dev(x + 1, y, z, core), dev(x + 3, y, z, core), dev(x + 2, y, z, core)
    mate = dev(x, y, z, 1 - core)

    barrier = pltpu.get_barrier_semaphore()

    def greet(j, carry):
        pl.semaphore_signal(barrier, inc=1, device_id=(peer(j, 1), batch), device_id_type=MESH)
        return carry

    lax.fori_loop(1, 16, greet, 0)
    for to in (zp, zm, zp2, zm2, yp, ym, y2):
        pl.semaphore_signal(barrier, inc=1, device_id=to, device_id_type=MESH)

    offs = (0, 3, 1, 2)

    def slot(dy, k):
        return ((y + dy) % 4) * 4 + (zl + offs[k]) % 4

    own_slot = slot(0, 0)
    mine = pl.ds(pl.multiple_of(core * CH, CH), CH)
    keeps = []
    for q in range(4):
        for n, (src, at, size, to) in enumerate(
            ((win, 384 * q, 384, 0), (wout, 1024 + 128 * q, 128, 384))
        ):
            keeps.append(
                pltpu.make_async_copy(
                    src.at[mine, pl.ds(at, size)], w_all.at[q, own_slot, :, pl.ds(to, size)], loc.at[q, n]
                )
            )
    keeps.append(
        pltpu.make_async_copy(
            wout.at[mine, pl.ds(pl.multiple_of(256 * x, 128), 256)], w_all.at[x, own_slot, :, pl.ds(512, 256)], loc.at[2, 3]
        )
    )
    for copy in keeps:
        copy.start()

    def rows(i):
        return pl.ds(pl.multiple_of(i * CH, CH), CH)

    def norm(load, gain_at, write):
        def add(i, acc):
            return acc + jnp.sum(load(i).reshape(CH // 8, 8, TOK), axis=0)

        total = lax.fori_loop(0, 16, add, jnp.zeros((8, TOK), F32))
        mean = jnp.sum(total, axis=0, keepdims=True) * (1.0 / D)

        def add_square(i, acc):
            c = load(i) - mean
            return acc + jnp.sum((c * c).reshape(CH // 8, 8, TOK), axis=0)

        total = lax.fori_loop(0, 16, add_square, jnp.zeros((8, TOK), F32))
        var = jnp.sum(total, axis=0, keepdims=True) * (1.0 / D)
        scale = lax.rsqrt(var + 1e-05)

        def finish(i):
            v = vecs[rows(i), :]
            c = load(i) - mean
            gain, shift = v[:, gain_at : gain_at + 1], v[:, gain_at + 1 : gain_at + 2]
            write(i, (c * scale * gain + shift).astype(BF16))

        loop(16, finish)

    def load_fields(i):
        return fields[rows(i), :].astype(F32)

    def write_normed(i, v):
        normed[rows(i), :] = v

    with jax.named_scope("norm1"):
        norm(load_fields, 0, write_normed)
    with jax.named_scope("greet_wait"):
        pl.semaphore_wait(barrier, 22)

    def to_block(j):
        return remote(
            normed.at[rows(peer(j, 1))], recv1.at[chan, pl.ds(0, CH)], s1.at[j], r1.at[j], (peer(j, 1), batch)
        )

    def from_plane(j):
        return remote(
            normed.at[rows(chan)], recv1.at[peer(j, -1), pl.ds(0, CH)], s1.at[j], r1.at[j], (peer(j, 1), batch)
        )

    first, last = pl.ds(0, 512), pl.ds(512, 256)

    def z_move(k, came):
        at = w_all.at[x, slot(0, k if came else 0)]
        to = {1: zp, 2: zm, 3: dev(x, y, z + 2 + 4 * core, core)}[k]
        return remote(at, at, zws.at[k], zwr.at[k], to)

    def x_move(k, way, came):
        at = w_all.at[(x + ((3, 1, 2)[way] if came else 0)) % 4, slot(0, k), :, first]
        return remote(at, at, xs.at[way, k], xr.at[way, k], (xp, xm, x2)[way])

    def y_move(k, way, came):
        at = w_all.at[:, slot((3, 1)[way] if came else 0, k), :, first]
        return remote(at, at, ys.at[way, k], yr.at[way, k], (yp, ym)[way])

    def y_pass(k, came):
        at = w_all.at[:, slot(2 if came else (3 if k < 2 else 1), k), :, first]
        return remote(at, at, y2s.at[k], y2r.at[k], yp if k < 2 else ym)

    def group(q, dy):
        return w_all.at[q, pl.ds(((y + dy) % 4) * 4, 4), :, last]

    def ay(r, came):
        at = group(x, offs[r] if came else 0)
        return remote(at, at, ays.at[r], ayr.at[r], {1: yp, 2: ym, 3: y2}[r])

    def ax(r, way, came):
        at = group((x + ((3, 1)[way] if came else 0)) % 4, offs[r])
        return remote(at, at, axs.at[way, r], axr.at[way, r], (xp, xm)[way])

    def ax_pass(r, came):
        at = group((x + (2 if came else (3 if r < 2 else 1))) % 4, offs[r])
        return remote(at, at, ax2s.at[r], ax2r.at[r], xp if r < 2 else xm)

    for copy in keeps:
        copy.wait()
    for k in (1, 2, 3):
        z_move(k, False).start()
    with jax.named_scope("blocks_send"):
        loop(15, lambda i: to_block(15 - i).start())
    keep = pltpu.make_async_copy(normed.at[rows(chan)], recv1.at[chan, pl.ds(0, CH)], loc.at[0, 3])
    keep.start()

    def start_y(k):
        y_move(k, 0, False).start()
        y_move(k, 1, False).start()

    start_y(0)

    def service_z():
        for k in (1, 2, 3):
            z_move(k, True).wait_recv()
            for way in range(3):
                x_move(k, way, False).start()
        for r in (1, 2, 3):
            ay(r, False).start()
        ax(0, 0, False).start()
        ax(0, 1, False).start()

    def service_y0():
        y_move(0, 0, True).wait_recv()
        y_pass(0, False).start()

    def service_x():
        for k in (1, 2, 3):
            for way in range(3):
                x_move(k, way, True).wait_recv()
            start_y(k)

    def service_a():
        for r in (1, 2, 3):
            ay(r, True).wait_recv()
            ax(r, 0, False).start()
            ax(r, 1, False).start()

    def service_y1():
        y_move(1, 0, True).wait_recv()
        y_pass(1, False).start()

    def service_y2():
        for k in (2, 3):
            y_move(k, 1, True).wait_recv()
            y_pass(k, False).start()

    def service_ax():
        for r in (0, 1):
            ax(r, 0, True).wait_recv()
            ax_pass(r, False).start()
        for r in (2, 3):
            ax(r, 1, True).wait_recv()
            ax_pass(r, False).start()

    with jax.named_scope("service_z"):
        service_z()
    with jax.named_scope("service_y0"):
        service_y0()
    def clear(a):
        recv1[a, pl.ds(CH, 32), :] = jnp.zeros((32, TOK), BF16)
        back[a, :, pl.ds(128, 128)] = jnp.zeros((2 * CH, 128), F32)

    with jax.named_scope("clear"):
        loop(16, clear)

    keep.wait()
    with jax.named_scope("service_x"):
        service_x()
    with jax.named_scope("service_a"):
        service_a()
    with jax.named_scope("blocks_wait"):
        loop(15, lambda i: from_plane(15 - i).wait_recv())

    def planes(p):
        both = recv1[pl.ds(2 * p, 2)].reshape(256, TOK)
        plane[p] = dot_nt(fwd[...], both)

    with jax.named_scope("planes"):
        loop(8, planes)


    def lines(t):
        re_at = pl.ds(pl.multiple_of(t * 8, 8), 8)
        im_at = pl.ds(pl.multiple_of(MODES + t * 8, 8), 8)
        vals = []
        for a in range(16):
            lanes = pl.ds((a % 2) * 128, 128)
            vals.append((plane[a // 2, re_at, lanes], plane[a // 2, im_at, lanes]))
        for a, (re, im) in enumerate(fft_list(vals, -1)):
            lanes = pl.ds((a % 2) * 128, 128)
            plane[a // 2, re_at, lanes] = re
            plane[a // 2, im_at, lanes] = im

    with jax.named_scope("lines"):
        loop(18, lines)

    def mix(p):
        v = plane[p].astype(BF16)
        lhs = jnp.concatenate(
            [
                jnp.concatenate([v[:MODES, :128], v[MODES:, :128]], axis=1),
                jnp.concatenate([v[:MODES, 128:], v[MODES:, 128:]], axis=1),
            ],
            axis=0,
        )
        mid[...] = gelu(dot(lhs, mix1[...]) + bias1[...]).astype(BF16)
        for half in range(2):
            res = dot_nt(mix2[...], mid[pl.ds(half * MODES, MODES), :]) + bias2[...]
            back[2 * p + half, :, pl.ds(0, MODES)] = shrink(res)

    with jax.named_scope("mix"):
        loop(8, mix)

    def lines_back(t):
        re_at = pl.ds(pl.multiple_of((t // 2) * 8, 8), 8)
        im_at = pl.ds(pl.multiple_of(CH + (t // 2) * 8, 8), 8)
        lanes = pl.ds(pl.multiple_of((t % 2) * 128, 128), 128)
        vals = [(back[a, re_at, lanes], back[a, im_at, lanes]) for a in range(16)]
        for a, (re, im) in enumerate(fft_list(vals, 1)):
            back[a, re_at, lanes] = re
            back[a, im_at, lanes] = im

    with jax.named_scope("lines_back"):
        loop(24, lines_back)

    def planes_back(p):
        lhs = [
            jnp.concatenate([back[2 * p + i, :CH, :], back[2 * p + i, CH:, :]], axis=1).astype(BF16)
            for i in range(2)
        ]
        res = dot(jnp.concatenate(lhs, axis=0), inv[...])
        for i in range(2):
            v = res[i * CH : (i + 1) * CH] + recv1[2 * p + i, pl.ds(0, CH), :].astype(F32)
            fil[2 * p + i] = v.astype(BF16)

    with jax.named_scope("planes_back"):
        loop(8, planes_back)

    def to_plane(j):
        return remote(fil.at[peer(j, 1)], recv2.at[rows(chan)], s2.at[j], r2.at[j], (peer(j, 1), batch))

    def from_block(j):
        return remote(fil.at[chan], recv2.at[rows(peer(j, -1))], s2.at[j], r2.at[j], (peer(j, 1), batch))

    loop(15, lambda i: to_plane(15 - i).start())
    keep = pltpu.make_async_copy(fil.at[chan], recv2.at[rows(chan)], loc.at[1, 3])
    keep.start()
    with jax.named_scope("service_y1"):
        service_y1()
    with jax.named_scope("service_ax"):
        service_ax()
    with jax.named_scope("service_y2"):
        service_y2()
    keep.wait()
    with jax.named_scope("filtered_wait"):
        loop(15, lambda i: from_block(15 - i).wait_recv())

    def hidden(i):
        hid[rows(i), :] = load_fields(i) + recv2[rows(i), :].astype(F32)

    with jax.named_scope("hidden"):
        loop(16, hidden)

    def write_z(i, v):
        recv2[rows(i), :] = v

    def load_hidden(i):
        return hid[rows(i), :]

    with jax.named_scope("norm2"):
        norm(load_hidden, 2, write_z)

    eye = (
        lax.broadcasted_iota(jnp.int32, (TOK, TOK), 0) == lax.broadcasted_iota(jnp.int32, (TOK, TOK), 1)
    ).astype(F32).astype(BF16)

    def turn(i):
        at = pl.ds(pl.multiple_of(i * 256, 256), 256)
        zt[0, :, at] = dot_nt(eye, recv2[at, :]).astype(BF16)

    with jax.named_scope("turn"):
        loop(6, turn)
    send_z = remote(zt.at[0], zt.at[1], zs, zr, mate)
    send_z.start()

    def units(i, t):
        g = [(y + offs[2 * i + n]) % 4 for n in range(2)]
        w = jnp.concatenate(
            [
                jnp.concatenate([w_all[q, pl.ds(g[n] * 4, 4), :, :384].reshape(384, 384) for q in range(4)], axis=1)
                for n in range(2)
            ],
            axis=0,
        )
        res = dot_nt(zt[t], w)
        for n in range(2):
            at = pl.ds(pl.multiple_of(g[n] * 384, 128), 384)
            act[t, :, at] = gelu(res[:, n * 384 : (n + 1) * 384] + b_in[:, at]).astype(BF16)

    with jax.named_scope("win_wait_a"):
        for k in (2, 3):
            y_move(k, 0, True).wait_recv()
    with jax.named_scope("units_own_a"):
        units(0, 0)
    with jax.named_scope("z_wait"):
        send_z.wait_recv()
    with jax.named_scope("units_mate_a"):
        units(0, 1)
    with jax.named_scope("win_wait_b"):
        for k in (0, 1):
            y_move(k, 1, True).wait_recv()
        for k in range(4):
            y_pass(k, True).wait_recv()
    with jax.named_scope("units_mate_b"):
        units(1, 1)
    with jax.named_scope("units_own_b"):
        units(1, 0)
    with jax.named_scope("wout_wait"):
        for r in range(4):
            ax(r, 0 if r >= 2 else 1, True).wait_recv()
        for r in range(4):
            ax_pass(r, True).wait_recv()

    def project(t, write):
        def one(q):
            write(
                pl.ds(pl.multiple_of(q * 256, 128), 256), dot(act[t], w_all[q, :, :, 512:].reshape(D, 256))
            )

        def two(i):
            w = jnp.concatenate([w_all[2 * i + n, :, :, 384:512].reshape(D, 128) for n in range(2)], axis=1)
            write(pl.ds(pl.multiple_of(1024 + i * 256, 128), 256), dot(act[t], w))

        loop(2, two)
        loop(4, one)

    def write_part(at, v):
        part[:, at] = v.astype(BF16)

    def write_own(at, v):
        own_t[:, at] = v

    with jax.named_scope("project_mate"):
        project(1, write_part)
    send_part = remote(part, precv, ps, pr, mate)
    send_part.start()

    with jax.named_scope("project_own"):
        project(0, write_own)
    with jax.named_scope("part_wait"):
        send_part.wait_recv()

    def finish(i):
        at = pl.ds(pl.multiple_of(i * 128, 128), 128)
        total = (own_t[:, at] + precv[:, at].astype(F32)).T
        out[at, :] = (hid[at, :] + total + vecs[at, :][:, 4:5]).astype(BF16)

    with jax.named_scope("finish"):
        loop(12, finish)

    loop(15, lambda i: to_block(15 - i).wait_send())
    loop(15, lambda i: to_plane(15 - i).wait_send())
    send_z.wait_send()
    send_part.wait_send()
    for k in range(4):
        if k:
            z_move(k, False).wait_send()
            ay(k, False).wait_send()
            for way in range(3):
                x_move(k, way, False).wait_send()
        for way in range(2):
            y_move(k, way, False).wait_send()
            ax(k, way, False).wait_send()
        y_pass(k, False).wait_send()
        ax_pass(k, False).wait_send()


def blocks_matrix(w, b):
    def diag(m):
        zero = jnp.zeros((HALF, HALF), F32)
        top = jnp.concatenate([m[0], zero], axis=1)
        low = jnp.concatenate([zero, m[1]], axis=1)
        return jnp.concatenate([top, low], axis=0)

    re, im = diag(w[0]), diag(w[1])
    full = jnp.stack([jnp.stack([re, im]), jnp.stack([-im, re])])
    return full, b.reshape(2, CH)


def on_device(
    fields, norm1_gain, norm1_shift, spec_w1, spec_b1, spec_w2, spec_b2,
    norm2_gain, norm2_shift, w_in, b_in, w_out, b_out,
):
    core = lax.axis_index("chan") % 2
    forward, inverse = plane_tables()
    m1, c1 = blocks_matrix(spec_w1, spec_b1)
    m1 = jnp.pad(m1, ((0, 0), (0, 0), (0, 32), (0, 32))).transpose(0, 2, 1, 3).reshape(256, 256)
    c1 = jnp.pad(c1, ((0, 0), (0, 32))).reshape(1, 256)
    m2, c2 = blocks_matrix(spec_w2, spec_b2)
    m2 = jnp.pad(m2, ((0, 0), (0, 0), (0, 32), (0, 0))).transpose(1, 3, 0, 2).reshape(192, 256)
    c2 = c2.reshape(192, 1)
    vecs = jnp.stack([norm1_gain, norm1_shift, norm2_gain, norm2_shift, b_out], axis=1)
    units_bias = lax.dynamic_slice(b_in.reshape(16, 2, CH), (0, core, 0), (16, 1, CH)).reshape(1, D)
    vmem = pl.BlockSpec(memory_space=pltpu.VMEM)
    dma = pltpu.SemaphoreType.DMA
    res = pl.pallas_call(
        kernel,
        out_shape=jax.ShapeDtypeStruct((D, TOK), BF16),
        in_specs=[vmem] * 3 + [pl.BlockSpec(memory_space=pl.ANY)] * 2 + [vmem] * 6,
        out_specs=vmem,
        scratch_shapes=[
            pltpu.VMEM((D, TOK), BF16),
            pltpu.VMEM((16, 128, TOK), BF16),
            pltpu.VMEM((8, 2 * MODES, 256), F32),
            pltpu.VMEM((2 * MODES, 256), BF16),
            pltpu.VMEM((16, 2 * CH, 256), F32),
            pltpu.VMEM((16, CH, TOK), BF16),
            pltpu.VMEM((D, TOK), BF16),
            pltpu.VMEM((D, TOK), F32),
            pltpu.VMEM((2, TOK, D), BF16),
            pltpu.VMEM((2, TOK, D), BF16),
            pltpu.VMEM((TOK, D), BF16),
            pltpu.VMEM((TOK, D), BF16),
            pltpu.VMEM((TOK, D), F32),
            pltpu.VMEM((4, 16, CH, 768), BF16),
            dma((16,)), dma((16,)), dma((16,)), dma((16,)), dma((4, 4)),
            dma, dma, dma, dma,
            dma((4,)), dma((4,)), dma((3, 4)), dma((3, 4)), dma((2, 4)), dma((2, 4)), dma((4,)), dma((4,)),
            dma((4,)), dma((4,)), dma((2, 4)), dma((2, 4)), dma((4,)), dma((4,)),
        ],
        compiler_params=pltpu.CompilerParams(
            collective_id=0, has_side_effects=True, vmem_limit_bytes=56 * 2**20
        ),
        name="block",
    )(
        fields[0], vecs, units_bias, w_in.T, w_out, m1.astype(BF16), m2.astype(BF16), c1, c2, forward, inverse
    )
    return res[None]


def solution(mesh):
    return jax.shard_map(
        on_device,
        mesh=mesh,
        in_specs=(
            P("batch", None, "chan"),
            P(),
            P(),
            P(None, "chan", None, None),
            P(None, "chan", None),
            P(None, "chan", None, None),
            P(None, "chan", None),
            P(),
            P(),
            P(None, "batch"),
            P(),
            P("batch", None),
            P(),
        ),
        out_specs=P("batch", None, "chan"),
        check_vma=False,
    )
```

```python
import math

import jax
import jax.numpy as jnp
import numpy as np
from jax import lax
from jax.experimental import pallas as pl
from jax.experimental.pallas import tpu as pltpu
from jax.sharding import PartitionSpec as P

D = 1536
TOK = 256
CH = 96
HALF = 48
GRID = 16
MODES = 144
SHRINK = 0.2
MESH = pl.DeviceIdType.MESH
F32 = jnp.float32
BF16 = jnp.bfloat16


def plane_tables():
    pos = np.arange(GRID)
    freq = np.arange(GRID // 2 + 1)
    phase = (
        pos[:, None, None, None] * pos[None, None, :, None]
        + pos[None, :, None, None] * freq[None, None, None, :]
    ) % GRID
    angle = phase * (2.0 * math.pi / GRID)
    cos = np.cos(angle).reshape(TOK, MODES) / 64.0
    sin = np.sin(angle).reshape(TOK, MODES) / 64.0
    weight = np.tile(np.where((freq == 0) | (freq == GRID // 2), 1.0, 2.0), GRID)
    forward = np.concatenate([cos, -sin], axis=1).T
    inverse = np.zeros((512, TOK))
    inverse[:MODES] = (cos * weight).T
    inverse[256 : 256 + MODES] = -(sin * weight).T
    return jnp.asarray(forward, F32), jnp.asarray(inverse, F32)


def turned(value, step, sign):
    re, im = value
    step = step % 16
    if step == 0:
        return value
    if step == 8:
        return (-re, -im)
    if step == 4:
        return (-im, re) if sign > 0 else (im, -re)
    if step == 12:
        return (im, -re) if sign > 0 else (-im, re)
    c = math.cos(2.0 * math.pi * step / 16)
    s = sign * math.sin(2.0 * math.pi * step / 16)
    return (re * c - im * s, re * s + im * c)


def fft_list(values, sign):
    n = len(values)
    if n == 1:
        return values
    even = fft_list(values[0::2], sign)
    odd = fft_list(values[1::2], sign)
    out = [None] * n
    for k in range(n // 2):
        t = turned(odd[k], k * (16 // n), sign)
        e = even[k]
        out[k] = (e[0] + t[0], e[1] + t[1])
        out[k + n // 2] = (e[0] - t[0], e[1] - t[1])
    return out


def gelu(v):
    size = jnp.abs(v)
    d = 1.0 + (0.3275911 * 0.7071067811865476) * size
    t = pl.reciprocal(d, approx=True)
    t = t * (2.0 - d * t)
    e = jnp.exp2(v * v * (-0.5 * 1.4426950408889634))
    q = 0.5 * 1.061405429 * t - 0.5 * 1.453152027
    q = q * t + 0.5 * 1.421413741
    q = q * t - 0.5 * 0.284496736
    q = q * t + 0.5 * 0.254829592
    return jnp.maximum(v, 0.0) - (q * t) * (e * size)


def shrink(v):
    return v - jnp.clip(v, -SHRINK, SHRINK)


def dot_nt(a, b):
    return lax.dot_general(a, b, (((1,), (1,)), ((), ())), preferred_element_type=F32)


def dot(a, b):
    return jnp.dot(a, b, preferred_element_type=F32)


def loop(n, body, unroll=1, start=0):
    def step(i, carry):
        body(i)
        return carry

    lax.fori_loop(start, n, step, 0, unroll=unroll)


def kernel(
    fields, gain1, shift1, gain2, shift2, b_out, b_in, win, wout, w1, b1, w2, b2, fwd_table, inv_table, out,
    normed, recv1, plane, mid, back, fil, recv2, hid, zt, act, part, precv, own_t,
    w_all, tile, row, mix1, mix2, bias1, bias2, units_bias, fwd, inv,
    s1, r1, s2, r2, loc, zs, zr, ps, pr,
    zws, zwr, xs, xr, ys, yr, y2s, y2r, ays, ayr, axs, axr, ax2s, ax2r,
):
    chan = lax.axis_index("chan")
    batch = lax.axis_index("batch")
    x, zh, core = chan // 4, (chan // 2) % 2, chan % 2
    y, zl = batch // 4, batch % 4
    z = zh * 4 + zl

    def dev(xx, yy, zz, cc):
        xx, yy, zz = xx % 4, yy % 4, zz % 8
        return ((xx * 2 + zz // 4) * 2 + cc, yy * 4 + zz % 4)

    def remote(src, dst, ss, rs, to):
        return pltpu.make_async_remote_copy(
            src_ref=src, dst_ref=dst, send_sem=ss, recv_sem=rs, device_id=to, device_id_type=MESH
        )

    def peer(j, way):
        dz, dx, dc = j // 8, (j // 2) % 4, j % 2
        px, pz, pc = (x + way * dx + 4) % 4, (zh + dz) % 2, (core + dc) % 2
        return (px * 2 + pz) * 2 + pc

    zp, zm = dev(x, y, z + 1, core), dev(x, y, z + 7, core)
    zp2, zm2 = dev(x, y, z + 2, core), dev(x, y, z + 6, core)
    yp, ym, y2 = dev(x, y + 1, z, core), dev(x, y + 3, z, core), dev(x, y + 2, z, core)
    xp, xm, x2 = dev(x + 1, y, z, core), dev(x + 3, y, z, core), dev(x + 2, y, z, core)
    mate = dev(x, y, z, 1 - core)

    barrier = pltpu.get_barrier_semaphore()

    def greet(j, carry):
        pl.semaphore_signal(barrier, inc=1, device_id=(peer(j, 1), batch), device_id_type=MESH)
        return carry

    lax.fori_loop(1, 16, greet, 0)
    for to in (zp, zm, zp2, zm2, yp, ym, y2):
        pl.semaphore_signal(barrier, inc=1, device_id=to, device_id_type=MESH)

    offs = (0, 3, 1, 2)

    def slot(dy, k):
        return ((y + dy) % 4) * 4 + (zl + offs[k]) % 4

    own_slot = slot(0, 0)
    mine = pl.ds(pl.multiple_of(core * CH, CH), CH)
    keeps = []
    for q in range(4):
        for n, (src, at, size, to) in enumerate(
            ((win, 384 * q, 384, 0), (wout, 1024 + 128 * q, 128, 384))
        ):
            keeps.append(
                pltpu.make_async_copy(
                    src.at[mine, pl.ds(at, size)], w_all.at[q, own_slot, :, pl.ds(to, size)], loc.at[q, n]
                )
            )
    keeps.append(
        pltpu.make_async_copy(
            wout.at[mine, pl.ds(pl.multiple_of(256 * x, 128), 256)], w_all.at[x, own_slot, :, pl.ds(512, 256)], loc.at[2, 3]
        )
    )
    for copy in keeps:
        copy.start()

    tile[...] = jnp.zeros_like(tile)
    row[...] = jnp.zeros_like(row)

    def diagonal(w, ri):
        tile[0, pl.ds(0, HALF), pl.ds(0, HALF)] = w[ri, 0]
        tile[1, pl.ds(HALF, HALF), pl.ds(0, HALF)] = w[ri, 1]
        return tile[0] + pltpu.roll(tile[1], HALF, 1)

    def bias_row(b, ri):
        row[pl.ds(0, 1), pl.ds(0, HALF)] = b[ri, pl.ds(0, 1)]
        row[pl.ds(8, 1), pl.ds(0, HALF)] = b[ri, pl.ds(1, 1)]
        both = row[pl.ds(0, 8), :] + pltpu.roll(row[pl.ds(8, 8), :], HALF, 1)
        return both[0:1]

    low, high = pl.ds(0, 128), pl.ds(128, 128)
    re, im = diagonal(w1, 0), diagonal(w1, 1)
    mix1[low, low], mix1[low, high] = re.astype(BF16), im.astype(BF16)
    mix1[high, low], mix1[high, high] = (-im).astype(BF16), re.astype(BF16)
    re, im = diagonal(w2, 0).T[:CH], diagonal(w2, 1).T[:CH]
    mix2[pl.ds(0, CH), low], mix2[pl.ds(0, CH), high] = re.astype(BF16), (-im).astype(BF16)
    mix2[pl.ds(CH, CH), low], mix2[pl.ds(CH, CH), high] = im.astype(BF16), re.astype(BF16)
    for ri in range(2):
        bias1[:, pl.ds(128 * ri, 128)] = bias_row(b1, ri)
        down = jnp.broadcast_to(bias_row(b2, ri), (128, 128)).T[:CH]
        bias2[pl.ds(CH * ri, CH), low] = down
        bias2[pl.ds(CH * ri, CH), pl.ds(128, 16)] = down[:, :16]

    fwd[...] = fwd_table[...].astype(BF16)
    inv[...] = inv_table[...].astype(BF16)
    lane = lax.broadcasted_iota(jnp.int32, (1, 768), 1)
    for g in range(4):
        six = jnp.concatenate([b_in[pl.ds(6 * g + i, 1), :] for i in range(6)], axis=1)
        six = jnp.where(core == 0, six, pltpu.roll(six, 768 - CH, 1))
        half = six
        for k in (1, 2, 3):
            half = jnp.where(lane < CH * k, half, pltpu.roll(six, 768 - CH * k, 1))
        units_bias[g, pl.ds(0, 1), :] = half[:, :384]

    def rows(i):
        return pl.ds(pl.multiple_of(i * CH, CH), CH)

    def chunk(i):
        return pl.ds(pl.multiple_of(i * 128, 128), 128)

    def column(vec, i):
        return jnp.broadcast_to(vec[pl.ds(i, 1), :], (128, 128)).T

    def norm(load, gains, shifts, write):
        def add(i, acc):
            return acc + jnp.sum(load(i).reshape(16, 8, TOK), axis=0)

        total = lax.fori_loop(0, 12, add, jnp.zeros((8, TOK), F32))
        mean = jnp.sum(total, axis=0, keepdims=True) * (1.0 / D)

        def add_square(i, acc):
            c = load(i) - mean
            return acc + jnp.sum((c * c).reshape(16, 8, TOK), axis=0)

        total = lax.fori_loop(0, 12, add_square, jnp.zeros((8, TOK), F32))
        var = jnp.sum(total, axis=0, keepdims=True) * (1.0 / D)
        scale = lax.rsqrt(var + 1e-05)

        def finish(i):
            c = (load(i) - mean) * scale
            gain, shift = column(gains, i), column(shifts, i)
            for at in (slice(0, 128), slice(128, 256)):
                write(i, at, (c[:, at] * gain + shift).astype(BF16))

        loop(12, finish)

    def load_fields(i):
        return fields[chunk(i), :].astype(F32)

    def write_normed(i, at, v):
        normed[chunk(i), at] = v

    with jax.named_scope("norm1"):
        norm(load_fields, gain1, shift1, write_normed)
    with jax.named_scope("greet_wait"):
        pl.semaphore_wait(barrier, 22)

    def to_block(j):
        return remote(
            normed.at[rows(peer(j, 1))], recv1.at[chan, pl.ds(0, CH)], s1.at[j], r1.at[j], (peer(j, 1), batch)
        )

    def from_plane(j):
        return remote(
            normed.at[rows(chan)], recv1.at[peer(j, -1), pl.ds(0, CH)], s1.at[j], r1.at[j], (peer(j, 1), batch)
        )

    first, last = pl.ds(0, 512), pl.ds(512, 256)

    def z_move(k, came):
        at = w_all.at[x, slot(0, k if came else 0)]
        to = {1: zp, 2: zm, 3: dev(x, y, z + 2 + 4 * core, core)}[k]
        return remote(at, at, zws.at[k], zwr.at[k], to)

    def x_move(k, way, came):
        at = w_all.at[(x + ((3, 1, 2)[way] if came else 0)) % 4, slot(0, k), :, first]
        return remote(at, at, xs.at[way, k], xr.at[way, k], (xp, xm, x2)[way])

    def y_move(k, way, came):
        at = w_all.at[:, slot((3, 1)[way] if came else 0, k), :, first]
        return remote(at, at, ys.at[way, k], yr.at[way, k], (yp, ym)[way])

    def y_pass(k, came):
        at = w_all.at[:, slot(2 if came else (3 if k < 2 else 1), k), :, first]
        return remote(at, at, y2s.at[k], y2r.at[k], yp if k < 2 else ym)

    def group(q, dy):
        return w_all.at[q, pl.ds(((y + dy) % 4) * 4, 4), :, last]

    def ay(r, came):
        at = group(x, offs[r] if came else 0)
        return remote(at, at, ays.at[r], ayr.at[r], {1: yp, 2: ym, 3: y2}[r])

    def ax(r, way, came):
        at = group((x + ((3, 1)[way] if came else 0)) % 4, offs[r])
        return remote(at, at, axs.at[way, r], axr.at[way, r], (xp, xm)[way])

    def ax_pass(r, came):
        at = group((x + (2 if came else (3 if r < 2 else 1))) % 4, offs[r])
        return remote(at, at, ax2s.at[r], ax2r.at[r], xp if r < 2 else xm)

    for copy in keeps:
        copy.wait()
    def start_z():
        for k in (1, 2, 3):
            z_move(k, False).start()

    with jax.named_scope("start_z"):
        start_z()
    with jax.named_scope("blocks_send"):
        loop(15, lambda i: to_block(15 - i).start())
    keep = pltpu.make_async_copy(normed.at[rows(chan)], recv1.at[chan, pl.ds(0, CH)], loc.at[0, 3])
    keep.start()

    def start_y(k):
        y_move(k, 0, False).start()
        y_move(k, 1, False).start()

    with jax.named_scope("start_y"):
        start_y(0)

    def service_z():
        for k in (1, 2, 3):
            z_move(k, True).wait_recv()
            for way in range(3):
                x_move(k, way, False).start()
        for r in (1, 2, 3):
            ay(r, False).start()
        ax(0, 0, False).start()
        ax(0, 1, False).start()

    def service_y0():
        y_move(0, 0, True).wait_recv()
        y_pass(0, False).start()

    def service_x():
        for k in (1, 2, 3):
            for way in range(3):
                x_move(k, way, True).wait_recv()
            start_y(k)

    def service_a():
        for r in (1, 2, 3):
            ay(r, True).wait_recv()
            ax(r, 0, False).start()
            ax(r, 1, False).start()

    def service_y1():
        y_move(1, 0, True).wait_recv()
        y_pass(1, False).start()

    def service_y2():
        for k in (2, 3):
            y_move(k, 1, True).wait_recv()
            y_pass(k, False).start()

    def service_ax():
        for r in (0, 1):
            ax(r, 0, True).wait_recv()
            ax_pass(r, False).start()
        for r in (2, 3):
            ax(r, 1, True).wait_recv()
            ax_pass(r, False).start()

    with jax.named_scope("service_z"):
        service_z()
    with jax.named_scope("service_y0"):
        service_y0()
    def clear(a):
        recv1[a, pl.ds(CH, 32), :] = jnp.zeros((32, TOK), BF16)
        back[a, :, pl.ds(128, 128)] = jnp.zeros((2 * CH, 128), F32)

    with jax.named_scope("clear"):
        loop(16, clear)

    keep.wait()
    with jax.named_scope("service_x"):
        service_x()
    with jax.named_scope("service_a"):
        service_a()
    def planes(p):
        both = recv1[pl.ds(2 * p, 2)].reshape(256, TOK)
        plane[p] = dot_nt(fwd[...], both)

    def planes_in(i):
        from_plane(2 * i).wait_recv()
        from_plane(2 * i + 1).wait_recv()
        planes(peer(2 * i, -1) // 2)

    with jax.named_scope("planes"):
        from_plane(1).wait_recv()
        planes(chan // 2)
        loop(8, planes_in, start=1)


    def lines(t):
        re_at = pl.ds(pl.multiple_of(t * 8, 8), 8)
        im_at = pl.ds(pl.multiple_of(MODES + t * 8, 8), 8)
        vals = []
        for a in range(16):
            lanes = pl.ds((a % 2) * 128, 128)
            vals.append((plane[a // 2, re_at, lanes], plane[a // 2, im_at, lanes]))
        for a, (re, im) in enumerate(fft_list(vals, -1)):
            lanes = pl.ds((a % 2) * 128, 128)
            plane[a // 2, re_at, lanes] = re
            plane[a // 2, im_at, lanes] = im

    with jax.named_scope("lines"):
        loop(18, lines, unroll=2)

    def mix(p):
        v = plane[p].astype(BF16)
        lhs = jnp.concatenate(
            [
                jnp.concatenate([v[:MODES, :128], v[MODES:, :128]], axis=1),
                jnp.concatenate([v[:MODES, 128:], v[MODES:, 128:]], axis=1),
            ],
            axis=0,
        )
        mid[...] = gelu(dot(lhs, mix1[...]) + bias1[...]).astype(BF16)
        for half in range(2):
            res = dot_nt(mix2[...], mid[pl.ds(half * MODES, MODES), :]) + bias2[...]
            back[2 * p + half, :, pl.ds(0, MODES)] = shrink(res)

    with jax.named_scope("mix"):
        loop(8, mix)

    def lines_back(t):
        re_at = pl.ds(pl.multiple_of((t // 2) * 8, 8), 8)
        im_at = pl.ds(pl.multiple_of(CH + (t // 2) * 8, 8), 8)
        lanes = pl.ds(pl.multiple_of((t % 2) * 128, 128), 128)
        vals = [(back[a, re_at, lanes], back[a, im_at, lanes]) for a in range(16)]
        for a, (re, im) in enumerate(fft_list(vals, 1)):
            back[a, re_at, lanes] = re
            back[a, im_at, lanes] = im

    with jax.named_scope("lines_back"):
        loop(24, lines_back, unroll=2)

    def planes_back(p):
        lhs = [
            jnp.concatenate([back[2 * p + i, :CH, :], back[2 * p + i, CH:, :]], axis=1).astype(BF16)
            for i in range(2)
        ]
        res = dot(jnp.concatenate(lhs, axis=0), inv[...])
        for i in range(2):
            v = res[i * CH : (i + 1) * CH] + recv1[2 * p + i, pl.ds(0, CH), :].astype(F32)
            fil[2 * p + i] = v.astype(BF16)

    def to_plane(j):
        return remote(fil.at[peer(j, 1)], recv2.at[rows(chan)], s2.at[j], r2.at[j], (peer(j, 1), batch))

    def from_block(j):
        return remote(fil.at[chan], recv2.at[rows(peer(j, -1))], s2.at[j], r2.at[j], (peer(j, 1), batch))

    def planes_out(i):
        planes_back(peer(14 - 2 * i, 1) // 2)
        to_plane(14 - 2 * i).start()
        to_plane(15 - 2 * i).start()

    with jax.named_scope("planes_back"):
        loop(7, planes_out)
        planes_back(chan // 2)
    to_plane(1).start()
    keep = pltpu.make_async_copy(fil.at[chan], recv2.at[rows(chan)], loc.at[1, 3])
    keep.start()
    with jax.named_scope("service_y1"):
        service_y1()
    with jax.named_scope("service_ax"):
        service_ax()
    with jax.named_scope("service_y2"):
        service_y2()
    keep.wait()
    with jax.named_scope("filtered_wait"):
        loop(15, lambda i: from_block(15 - i).wait_recv())

    def hidden(i):
        hid[chunk(i), :] = load_fields(i) + recv2[chunk(i), :].astype(F32)

    with jax.named_scope("hidden"):
        loop(12, hidden)

    def write_z(i, at, v):
        recv2[chunk(i), at] = v

    def load_hidden(i):
        return hid[chunk(i), :]

    with jax.named_scope("norm2"):
        norm(load_hidden, gain2, shift2, write_z)

    eye = (
        lax.broadcasted_iota(jnp.int32, (TOK, TOK), 0) == lax.broadcasted_iota(jnp.int32, (TOK, TOK), 1)
    ).astype(F32).astype(BF16)

    def turn(i):
        at = pl.ds(pl.multiple_of(i * 256, 256), 256)
        zt[0, :, at] = dot_nt(eye, recv2[at, :]).astype(BF16)

    with jax.named_scope("turn"):
        loop(6, turn)
    send_z = remote(zt.at[0], zt.at[1], zs, zr, mate)
    send_z.start()

    def units(i, t):
        g = [(y + offs[2 * i + n]) % 4 for n in range(2)]
        w = jnp.concatenate(
            [
                jnp.concatenate([w_all[q, pl.ds(g[n] * 4, 4), :, :384].reshape(384, 384) for q in range(4)], axis=1)
                for n in range(2)
            ],
            axis=0,
        )
        res = dot_nt(zt[t], w)
        for n in range(2):
            at = pl.ds(pl.multiple_of(g[n] * 384, 128), 384)
            act[t, :, at] = gelu(res[:, n * 384 : (n + 1) * 384] + units_bias[g[n], pl.ds(0, 1), :]).astype(BF16)

    with jax.named_scope("win_wait_a"):
        for k in (2, 3):
            y_move(k, 0, True).wait_recv()
    with jax.named_scope("units_own_a"):
        units(0, 0)
    with jax.named_scope("z_wait"):
        send_z.wait_recv()
    with jax.named_scope("units_mate_a"):
        units(0, 1)
    with jax.named_scope("win_wait_b"):
        for k in (0, 1):
            y_move(k, 1, True).wait_recv()
        for k in range(4):
            y_pass(k, True).wait_recv()
    with jax.named_scope("units_mate_b"):
        units(1, 1)
    with jax.named_scope("units_own_b"):
        units(1, 0)
    with jax.named_scope("wout_wait"):
        for r in range(4):
            ax(r, 0 if r >= 2 else 1, True).wait_recv()
        for r in range(4):
            ax_pass(r, True).wait_recv()

    def project(t, write):
        def one(q):
            write(
                pl.ds(pl.multiple_of(q * 256, 128), 256), dot(act[t], w_all[q, :, :, 512:].reshape(D, 256))
            )

        def two(i):
            w = jnp.concatenate([w_all[2 * i + n, :, :, 384:512].reshape(D, 128) for n in range(2)], axis=1)
            write(pl.ds(pl.multiple_of(1024 + i * 256, 128), 256), dot(act[t], w))

        loop(2, two)
        loop(4, one)

    def write_part(at, v):
        part[:, at] = v.astype(BF16)

    def write_own(at, v):
        own_t[:, at] = v

    with jax.named_scope("project_mate"):
        project(1, write_part)
    send_part = remote(part, precv, ps, pr, mate)
    send_part.start()

    with jax.named_scope("project_own"):
        project(0, write_own)
    with jax.named_scope("part_wait"):
        send_part.wait_recv()

    def finish(i):
        at = pl.ds(pl.multiple_of(i * 128, 128), 128)
        total = (own_t[:, at] + precv[:, at].astype(F32)).T
        shift = column(b_out, i)
        for to in (slice(0, 128), slice(128, 256)):
            out[at, to] = (hid[at, to] + total[:, to] + shift).astype(BF16)

    with jax.named_scope("finish"):
        loop(12, finish)

    loop(15, lambda i: to_block(15 - i).wait_send())
    loop(15, lambda i: to_plane(15 - i).wait_send())
    send_z.wait_send()
    send_part.wait_send()
    def sent():
        for k in range(4):
            if k:
                z_move(k, False).wait_send()
                ay(k, False).wait_send()
                for way in range(3):
                    x_move(k, way, False).wait_send()
            for way in range(2):
                y_move(k, way, False).wait_send()
                ax(k, way, False).wait_send()
            y_pass(k, False).wait_send()
            ax_pass(k, False).wait_send()

    with jax.named_scope("sent"):
        sent()


def on_device(
    fields, norm1_gain, norm1_shift, spec_w1, spec_b1, spec_w2, spec_b2,
    norm2_gain, norm2_shift, w_in, b_in, w_out, b_out,
):
    forward, inverse = plane_tables()
    gain1, shift1, gain2, shift2, last = (
        v.reshape(12, 128) for v in (norm1_gain, norm1_shift, norm2_gain, norm2_shift, b_out)
    )
    vmem = pl.BlockSpec(memory_space=pltpu.VMEM)
    dma = pltpu.SemaphoreType.DMA
    res = pl.pallas_call(
        kernel,
        out_shape=jax.ShapeDtypeStruct((D, TOK), BF16),
        in_specs=[vmem] * 7 + [pl.BlockSpec(memory_space=pl.ANY)] * 2 + [vmem] * 6,
        out_specs=vmem,
        scratch_shapes=[
            pltpu.VMEM((D, TOK), BF16),
            pltpu.VMEM((16, 128, TOK), BF16),
            pltpu.VMEM((8, 2 * MODES, 256), F32),
            pltpu.VMEM((2 * MODES, 256), BF16),
            pltpu.VMEM((16, 2 * CH, 256), F32),
            pltpu.VMEM((16, CH, TOK), BF16),
            pltpu.VMEM((D, TOK), BF16),
            pltpu.VMEM((D, TOK), F32),
            pltpu.VMEM((2, TOK, D), BF16),
            pltpu.VMEM((2, TOK, D), BF16),
            pltpu.VMEM((TOK, D), BF16),
            pltpu.VMEM((TOK, D), BF16),
            pltpu.VMEM((TOK, D), F32),
            pltpu.VMEM((4, 16, CH, 768), BF16),
            pltpu.VMEM((2, 128, 128), F32),
            pltpu.VMEM((16, 128), F32),
            pltpu.VMEM((256, 256), BF16),
            pltpu.VMEM((2 * CH, 256), BF16),
            pltpu.VMEM((1, 256), F32),
            pltpu.VMEM((2 * CH, MODES), F32),
            pltpu.VMEM((4, 8, 384), F32),
            pltpu.VMEM((2 * MODES, TOK), BF16),
            pltpu.VMEM((512, TOK), BF16),
            dma((16,)), dma((16,)), dma((16,)), dma((16,)), dma((4, 4)),
            dma, dma, dma, dma,
            dma((4,)), dma((4,)), dma((3, 4)), dma((3, 4)), dma((2, 4)), dma((2, 4)), dma((4,)), dma((4,)),
            dma((4,)), dma((4,)), dma((2, 4)), dma((2, 4)), dma((4,)), dma((4,)),
        ],
        compiler_params=pltpu.CompilerParams(
            collective_id=0, has_side_effects=True, vmem_limit_bytes=56 * 2**20
        ),
        name="block",
    )(
        fields[0], gain1, shift1, gain2, shift2, last, b_in.reshape(24, 128), w_in.T, w_out,
        spec_w1, spec_b1, spec_w2, spec_b2, forward, inverse,
    )
    return res[None]


def solution(mesh):
    return jax.shard_map(
        on_device,
        mesh=mesh,
        in_specs=(
            P("batch", None, "chan"),
            P(),
            P(),
            P(None, "chan", None, None),
            P(None, "chan", None),
            P(None, "chan", None, None),
            P(None, "chan", None),
            P(),
            P(),
            P(None, "batch"),
            P(),
            P("batch", None),
            P(),
        ),
        out_specs=P("batch", None, "chan"),
        check_vma=False,
    )
```

```python
import math

import jax
import jax.numpy as jnp
import numpy as np
from jax import lax
from jax.experimental import pallas as pl
from jax.experimental.pallas import tpu as pltpu
from jax.sharding import PartitionSpec as P

D = 1536
TOK = 256
CH = 96
HALF = 48
GRID = 16
MODES = 144
SHRINK = 0.2
MESH = pl.DeviceIdType.MESH
F32 = jnp.float32
BF16 = jnp.bfloat16


def plane_tables():
    pos = np.arange(GRID)
    freq = np.arange(GRID // 2 + 1)
    phase = (
        pos[:, None, None, None] * pos[None, None, :, None]
        + pos[None, :, None, None] * freq[None, None, None, :]
    ) % GRID
    angle = phase * (2.0 * math.pi / GRID)
    cos = np.cos(angle).reshape(TOK, MODES) / 64.0
    sin = np.sin(angle).reshape(TOK, MODES) / 64.0
    weight = np.tile(np.where((freq == 0) | (freq == GRID // 2), 1.0, 2.0), GRID)
    forward = np.concatenate([cos, -sin], axis=1).T
    inverse = np.zeros((512, TOK))
    inverse[:MODES] = (cos * weight).T
    inverse[256 : 256 + MODES] = -(sin * weight).T
    return jnp.asarray(forward, F32), jnp.asarray(inverse, F32)


def turned(value, step, sign):
    re, im = value
    step = step % 16
    if step == 0:
        return value
    if step == 8:
        return (-re, -im)
    if step == 4:
        return (-im, re) if sign > 0 else (im, -re)
    if step == 12:
        return (im, -re) if sign > 0 else (-im, re)
    c = math.cos(2.0 * math.pi * step / 16)
    s = sign * math.sin(2.0 * math.pi * step / 16)
    return (re * c - im * s, re * s + im * c)


def fft_list(values, sign):
    n = len(values)
    if n == 1:
        return values
    even = fft_list(values[0::2], sign)
    odd = fft_list(values[1::2], sign)
    out = [None] * n
    for k in range(n // 2):
        t = turned(odd[k], k * (16 // n), sign)
        e = even[k]
        out[k] = (e[0] + t[0], e[1] + t[1])
        out[k + n // 2] = (e[0] - t[0], e[1] - t[1])
    return out


def gelu(v):
    size = jnp.abs(v)
    d = 1.0 + (0.3275911 * 0.7071067811865476) * size
    t = pl.reciprocal(d, approx=True)
    t = t * (2.0 - d * t)
    e = jnp.exp2(v * v * (-0.5 * 1.4426950408889634))
    q = 0.5 * 1.061405429 * t - 0.5 * 1.453152027
    q = q * t + 0.5 * 1.421413741
    q = q * t - 0.5 * 0.284496736
    q = q * t + 0.5 * 0.254829592
    return jnp.maximum(v, 0.0) - (q * t) * (e * size)


def shrink(v):
    return v - jnp.clip(v, -SHRINK, SHRINK)


def dot_nt(a, b):
    return lax.dot_general(a, b, (((1,), (1,)), ((), ())), preferred_element_type=F32)


def dot(a, b):
    return jnp.dot(a, b, preferred_element_type=F32)


def loop(n, body, unroll=1, start=0):
    def step(i, carry):
        body(i)
        return carry

    lax.fori_loop(start, n, step, 0, unroll=unroll)


def kernel(
    fields, gain1, shift1, gain2, shift2, b_out, b_in, win, wout, w1, b1, w2, b2, fwd_table, inv_table, out,
    normed, recv1, plane, mid, back, fil, recv2, hid, zt, act, part, precv, own_t,
    w_wide, w_slim, tile, row, mix1, mix2, bias1, bias2, units_bias, fwd, inv,
    s1, r1, s2, r2, loc, zs, zr, ps, pr,
    zws, zwr, xs, xr, ys, yr, y2s, y2r, ays, ayr, axs, axr, ax2s, ax2r,
):
    chan = lax.axis_index("chan")
    batch = lax.axis_index("batch")
    x, zh, core = chan // 4, (chan // 2) % 2, chan % 2
    y, zl = batch // 4, batch % 4
    z = zh * 4 + zl

    def dev(xx, yy, zz, cc):
        xx, yy, zz = xx % 4, yy % 4, zz % 8
        return ((xx * 2 + zz // 4) * 2 + cc, yy * 4 + zz % 4)

    def remote(src, dst, ss, rs, to):
        return pltpu.make_async_remote_copy(
            src_ref=src, dst_ref=dst, send_sem=ss, recv_sem=rs, device_id=to, device_id_type=MESH
        )

    def peer(j, way):
        dz, dx, dc = j // 8, (j // 2) % 4, j % 2
        px, pz, pc = (x + way * dx + 4) % 4, (zh + dz) % 2, (core + dc) % 2
        return (px * 2 + pz) * 2 + pc

    zp, zm = dev(x, y, z + 1, core), dev(x, y, z + 7, core)
    zp2, zm2 = dev(x, y, z + 2, core), dev(x, y, z + 6, core)
    yp, ym, y2 = dev(x, y + 1, z, core), dev(x, y + 3, z, core), dev(x, y + 2, z, core)
    xp, xm, x2 = dev(x + 1, y, z, core), dev(x + 3, y, z, core), dev(x + 2, y, z, core)
    mate = dev(x, y, z, 1 - core)

    barrier = pltpu.get_barrier_semaphore()

    def greet(j, carry):
        pl.semaphore_signal(barrier, inc=1, device_id=(peer(j, 1), batch), device_id_type=MESH)
        return carry

    lax.fori_loop(1, 16, greet, 0)
    for to in (zp, zm, zp2, zm2, yp, ym, y2):
        pl.semaphore_signal(barrier, inc=1, device_id=to, device_id_type=MESH)

    offs = (0, 3, 1, 2)

    def slot(dy, k):
        return ((y + dy) % 4) * 4 + (zl + offs[k]) % 4

    own_slot = slot(0, 0)
    mine = pl.ds(pl.multiple_of(core * CH, CH), CH)
    keeps = []
    for ph, src in enumerate((win, wout)):
        for q in range(4):
            keeps.append(
                pltpu.make_async_copy(src.at[mine, pl.ds(384 * q, 256)], w_wide.at[ph, q, own_slot], loc.at[ph, q])
            )
        at = pl.ds(pl.multiple_of(384 * x + 256, 128), 128)
        keeps.append(pltpu.make_async_copy(src.at[mine, at], w_slim.at[ph, x, own_slot], loc.at[ph, 4]))
    for copy in keeps:
        copy.start()

    def rows(i):
        return pl.ds(pl.multiple_of(i * CH, CH), CH)

    def chunk(i):
        return pl.ds(pl.multiple_of(i * 128, 128), 128)

    def column(vec, i):
        return jnp.broadcast_to(vec[pl.ds(i, 1), :], (128, 128)).T

    def norm(load, gains, shifts, write, total=None):
        def add(i, acc):
            return acc + jnp.sum(load(i).reshape(16, 8, TOK), axis=0)

        if total is None:
            total = lax.fori_loop(0, 12, add, jnp.zeros((8, TOK), F32))
        mean = jnp.sum(total, axis=0, keepdims=True) * (1.0 / D)

        def add_square(i, acc):
            c = load(i) - mean
            return acc + jnp.sum((c * c).reshape(16, 8, TOK), axis=0)

        total = lax.fori_loop(0, 12, add_square, jnp.zeros((8, TOK), F32))
        var = jnp.sum(total, axis=0, keepdims=True) * (1.0 / D)
        scale = lax.rsqrt(var + 1e-05)

        def finish(i):
            c = (load(i) - mean) * scale
            gain, shift = column(gains, i), column(shifts, i)
            for at in (slice(0, 128), slice(128, 256)):
                write(i, at, (c[:, at] * gain + shift).astype(BF16))

        loop(12, finish)

    def load_fields(i):
        return fields[chunk(i), :].astype(F32)

    def write_normed(i, at, v):
        normed[chunk(i), at] = v

    with jax.named_scope("norm1"):
        norm(load_fields, gain1, shift1, write_normed)
    with jax.named_scope("greet_wait"):
        pl.semaphore_wait(barrier, 22)

    def to_block(j):
        return remote(
            normed.at[rows(peer(j, 1))], recv1.at[chan, pl.ds(0, CH)], s1.at[j], r1.at[j], (peer(j, 1), batch)
        )

    def from_plane(j):
        return remote(
            normed.at[rows(chan)], recv1.at[peer(j, -1), pl.ds(0, CH)], s1.at[j], r1.at[j], (peer(j, 1), batch)
        )

    def z_move(ph, k, wide, came):
        ref = w_wide if wide else w_slim
        at = ref.at[ph, x, slot(0, k if came else 0)]
        to = {1: zp, 2: zm, 3: dev(x, y, z + 2 + 4 * core, core)}[k]
        return remote(at, at, zws.at[ph, wide, k], zwr.at[ph, wide, k], to)

    def x_move(ph, k, way, came):
        at = w_wide.at[ph, (x + ((3, 1, 2)[way] if came else 0)) % 4, slot(0, k)]
        return remote(at, at, xs.at[ph, way, k], xr.at[ph, way, k], (xp, xm, x2)[way])

    def y_move(ph, k, way, came):
        at = w_wide.at[ph, :, slot((3, 1)[way] if came else 0, k)]
        return remote(at, at, ys.at[ph, way, k], yr.at[ph, way, k], (yp, ym)[way])

    def y_pass(ph, k, came):
        at = w_wide.at[ph, :, slot(2 if came else (3 if k < 2 else 1), k)]
        return remote(at, at, y2s.at[ph, k], y2r.at[ph, k], yp if k < 2 else ym)

    def group(ph, q, dy):
        return w_slim.at[ph, q, pl.ds(((y + dy) % 4) * 4, 4)]

    def ay(ph, r, came):
        at = group(ph, x, offs[r] if came else 0)
        return remote(at, at, ays.at[ph, r], ayr.at[ph, r], {1: yp, 2: ym, 3: y2}[r])

    def ax(ph, r, way, came):
        at = group(ph, (x + ((3, 1)[way] if came else 0)) % 4, offs[r])
        return remote(at, at, axs.at[ph, way, r], axr.at[ph, way, r], (xp, xm)[way])

    def ax_pass(ph, r, came):
        at = group(ph, (x + (2 if came else (3 if r < 2 else 1))) % 4, offs[r])
        return remote(at, at, ax2s.at[ph, r], ax2r.at[ph, r], xp if r < 2 else xm)

    def start_z(ph):
        for k in (1, 2, 3):
            z_move(ph, k, 1, False).start()
            z_move(ph, k, 0, False).start()

    def start_y(ph, k):
        y_move(ph, k, 0, False).start()
        y_move(ph, k, 1, False).start()

    for copy in keeps:
        copy.wait()
    with jax.named_scope("start_z"):
        start_z(0)
        start_z(1)
    with jax.named_scope("blocks_send"):
        loop(8, lambda i: to_block(15 - i).start())
    keep = pltpu.make_async_copy(normed.at[rows(chan)], recv1.at[chan, pl.ds(0, CH)], loc.at[0, 5])
    keep.start()

    with jax.named_scope("start_y"):
        start_y(0, 0)
        start_y(1, 0)
    loop(7, lambda i: to_block(7 - i).start())

    def service_z(ph):
        for k in (1, 2, 3):
            z_move(ph, k, 1, True).wait_recv()
            for way in range(3):
                x_move(ph, k, way, False).start()
            z_move(ph, k, 0, True).wait_recv()
        for r in (1, 2, 3):
            ay(ph, r, False).start()
        ax(ph, 0, 0, False).start()
        ax(ph, 0, 1, False).start()

    def service_x(ph):
        for k in (1, 2, 3):
            for way in range(3):
                x_move(ph, k, way, True).wait_recv()
            start_y(ph, k)

    def service_a(ph):
        for r in (1, 2, 3):
            ay(ph, r, True).wait_recv()
            ax(ph, r, 0, False).start()
            ax(ph, r, 1, False).start()

    def service_y(ph, ks):
        for k in ks:
            y_move(ph, k, 0 if k < 2 else 1, True).wait_recv()
            y_pass(ph, k, False).start()

    def service_ax(ph):
        for r in range(4):
            ax(ph, r, 0 if r < 2 else 1, True).wait_recv()
            ax_pass(ph, r, False).start()

    with jax.named_scope("service_1"):
        service_z(0)
        service_y(0, (0,))
        service_z(1)
    tile[...] = jnp.zeros_like(tile)
    row[...] = jnp.zeros_like(row)

    def diagonal(w, ri):
        tile[0, pl.ds(0, HALF), pl.ds(0, HALF)] = w[ri, 0]
        tile[1, pl.ds(HALF, HALF), pl.ds(0, HALF)] = w[ri, 1]
        return tile[0] + pltpu.roll(tile[1], HALF, 1)

    def bias_row(b, ri):
        row[pl.ds(0, 1), pl.ds(0, HALF)] = b[ri, pl.ds(0, 1)]
        row[pl.ds(8, 1), pl.ds(0, HALF)] = b[ri, pl.ds(1, 1)]
        both = row[pl.ds(0, 8), :] + pltpu.roll(row[pl.ds(8, 8), :], HALF, 1)
        return both[0:1]

    low, high = pl.ds(0, 128), pl.ds(128, 128)
    re, im = diagonal(w1, 0), diagonal(w1, 1)
    mix1[low, low], mix1[low, high] = re.astype(BF16), im.astype(BF16)
    mix1[high, low], mix1[high, high] = (-im).astype(BF16), re.astype(BF16)
    re, im = diagonal(w2, 0).T[:CH], diagonal(w2, 1).T[:CH]
    mix2[pl.ds(0, CH), low], mix2[pl.ds(0, CH), high] = re.astype(BF16), (-im).astype(BF16)
    mix2[pl.ds(CH, CH), low], mix2[pl.ds(CH, CH), high] = im.astype(BF16), re.astype(BF16)
    for ri in range(2):
        bias1[:, pl.ds(128 * ri, 128)] = bias_row(b1, ri)
        down = jnp.broadcast_to(bias_row(b2, ri), (128, 128)).T[:CH]
        bias2[pl.ds(CH * ri, CH), low] = down
        bias2[pl.ds(CH * ri, CH), pl.ds(128, 16)] = down[:, :16]

    fwd[...] = fwd_table[...].astype(BF16)
    inv[...] = inv_table[...].astype(BF16)
    lane = lax.broadcasted_iota(jnp.int32, (1, 768), 1)
    for g in range(4):
        six = jnp.concatenate([b_in[pl.ds(6 * g + i, 1), :] for i in range(6)], axis=1)
        six = jnp.where(core == 0, six, pltpu.roll(six, 768 - CH, 1))
        half = six
        for k in (1, 2, 3):
            half = jnp.where(lane < CH * k, half, pltpu.roll(six, 768 - CH * k, 1))
        units_bias[g, pl.ds(0, 1), :] = half[:, :384]

    def clear(a):
        recv1[a, pl.ds(CH, 32), :] = jnp.zeros((32, TOK), BF16)
        back[a, :, pl.ds(128, 128)] = jnp.zeros((2 * CH, 128), F32)

    with jax.named_scope("clear"):
        loop(16, clear)

    keep.wait()
    with jax.named_scope("service_2"):
        service_x(0)
        service_a(0)
        service_y(1, (0,))

    with jax.named_scope("service_3"):
        service_x(1)
        service_y(0, (1,))

    def planes(p):
        both = recv1[pl.ds(2 * p, 2)].reshape(256, TOK)
        plane[p] = dot_nt(fwd[...], both)

    def planes_in(i):
        from_plane(2 * i).wait_recv()
        from_plane(2 * i + 1).wait_recv()
        planes(peer(2 * i, -1) // 2)

    with jax.named_scope("planes"):
        from_plane(1).wait_recv()
        planes(chan // 2)
        loop(8, planes_in, start=1)


    def lines(t):
        re_at = pl.ds(pl.multiple_of(t * 8, 8), 8)
        im_at = pl.ds(pl.multiple_of(MODES + t * 8, 8), 8)
        vals = []
        for a in range(16):
            lanes = pl.ds((a % 2) * 128, 128)
            vals.append((plane[a // 2, re_at, lanes], plane[a // 2, im_at, lanes]))
        for a, (re, im) in enumerate(fft_list(vals, -1)):
            lanes = pl.ds((a % 2) * 128, 128)
            plane[a // 2, re_at, lanes] = re
            plane[a // 2, im_at, lanes] = im

    with jax.named_scope("lines"):
        loop(18, lines, unroll=2)

    def mix_in(p):
        v = plane[p].astype(BF16)
        lhs = jnp.concatenate(
            [
                jnp.concatenate([v[:MODES, :128], v[MODES:, :128]], axis=1),
                jnp.concatenate([v[:MODES, 128:], v[MODES:, 128:]], axis=1),
            ],
            axis=0,
        )
        mid[p] = gelu(dot(lhs, mix1[...]) + bias1[...]).astype(BF16)

    def mix_out(p):
        for half in range(2):
            res = dot_nt(mix2[...], mid[p, pl.ds(half * MODES, MODES), :]) + bias2[...]
            back[2 * p + half, :, pl.ds(0, MODES)] = shrink(res)

    with jax.named_scope("mix"):
        loop(8, mix_in, unroll=2)
        loop(8, mix_out, unroll=2)
    with jax.named_scope("service_4"):
        service_y(0, (2, 3))
        service_a(1)

    def lines_back(t):
        re_at = pl.ds(pl.multiple_of((t // 2) * 8, 8), 8)
        im_at = pl.ds(pl.multiple_of(CH + (t // 2) * 8, 8), 8)
        lanes = pl.ds(pl.multiple_of((t % 2) * 128, 128), 128)
        vals = [(back[a, re_at, lanes], back[a, im_at, lanes]) for a in range(16)]
        for a, (re, im) in enumerate(fft_list(vals, 1)):
            back[a, re_at, lanes] = re
            back[a, im_at, lanes] = im

    with jax.named_scope("lines_back"):
        loop(24, lines_back, unroll=2)

    def planes_back(p):
        lhs = [
            jnp.concatenate([back[2 * p + i, :CH, :], back[2 * p + i, CH:, :]], axis=1).astype(BF16)
            for i in range(2)
        ]
        res = dot(jnp.concatenate(lhs, axis=0), inv[...])
        for i in range(2):
            v = res[i * CH : (i + 1) * CH] + recv1[2 * p + i, pl.ds(0, CH), :].astype(F32)
            fil[2 * p + i] = v.astype(BF16)

    def to_plane(j):
        return remote(fil.at[peer(j, 1)], recv2.at[rows(chan)], s2.at[j], r2.at[j], (peer(j, 1), batch))

    def from_block(j):
        return remote(fil.at[chan], recv2.at[rows(peer(j, -1))], s2.at[j], r2.at[j], (peer(j, 1), batch))

    def planes_out(i):
        planes_back(peer(14 - 2 * i, 1) // 2)
        to_plane(14 - 2 * i).start()
        to_plane(15 - 2 * i).start()

    with jax.named_scope("planes_back"):
        loop(7, planes_out)
        planes_back(chan // 2)
    to_plane(1).start()
    keep = pltpu.make_async_copy(fil.at[chan], recv2.at[rows(chan)], loc.at[1, 5])
    keep.start()
    with jax.named_scope("service_5"):
        service_y(1, (1,))
        service_ax(0)
        service_y(1, (2, 3))
        service_ax(1)
    keep.wait()

    def take(p, acc):
        v = fields[rows(p), :].astype(F32) + recv2[rows(p), :].astype(F32)
        hid[rows(p), :] = v
        return acc + jnp.sum(v.reshape(CH // 8, 8, TOK), axis=0)

    def take_next(j, acc):
        from_block(j).wait_recv()
        return take(peer(j, -1), acc)

    with jax.named_scope("filtered_wait"):
        channel_sum = lax.fori_loop(1, 16, take_next, take(chan, jnp.zeros((8, TOK), F32)))

    def write_z(i, at, v):
        recv2[chunk(i), at] = v

    def load_hidden(i):
        return hid[chunk(i), :]

    with jax.named_scope("norm2"):
        norm(load_hidden, gain2, shift2, write_z, channel_sum)

    eye = (
        lax.broadcasted_iota(jnp.int32, (TOK, TOK), 0) == lax.broadcasted_iota(jnp.int32, (TOK, TOK), 1)
    ).astype(F32).astype(BF16)

    def turn(i):
        at = pl.ds(pl.multiple_of(i * 256, 256), 256)
        zt[0, :, at] = dot_nt(eye, recv2[at, :]).astype(BF16)

    with jax.named_scope("turn"):
        loop(6, turn)
    send_z = remote(zt.at[0], zt.at[1], zs, zr, mate)
    send_z.start()

    def units(i, t):
        g = [(y + offs[2 * i + n]) % 4 for n in range(2)]

        def shards(n):
            at = pl.ds(g[n] * 4, 4)
            parts = [
                (w_wide[0, q, at].reshape(384, 256), w_slim[0, q, at].reshape(384, 128)) for q in range(4)
            ]
            return jnp.concatenate([v for pair in parts for v in pair], axis=1)

        res = dot_nt(zt[t], jnp.concatenate([shards(0), shards(1)], axis=0))
        for n in range(2):
            at = pl.ds(pl.multiple_of(g[n] * 384, 128), 384)
            act[t, :, at] = gelu(res[:, n * 384 : (n + 1) * 384] + units_bias[g[n], pl.ds(0, 1), :]).astype(BF16)

    def arrived(ph):
        for k in range(4):
            y_move(ph, k, 0 if k >= 2 else 1, True).wait_recv()
        for r in range(4):
            ax(ph, r, 0 if r >= 2 else 1, True).wait_recv()
        for k in range(4):
            ax_pass(ph, k, True).wait_recv()
        for k in range(4):
            y_pass(ph, k, True).wait_recv()

    with jax.named_scope("win_wait"):
        for k in (2, 3):
            y_move(0, k, 0, True).wait_recv()
        for r in range(4):
            ax(0, r, 0 if r >= 2 else 1, True).wait_recv()
        for k in range(4):
            ax_pass(0, k, True).wait_recv()
    with jax.named_scope("units_own_a"):
        units(0, 0)
    with jax.named_scope("win_wait_b"):
        for k in (0, 1):
            y_move(0, k, 1, True).wait_recv()
        for k in range(4):
            y_pass(0, k, True).wait_recv()
    with jax.named_scope("units_own_b"):
        units(1, 0)
    with jax.named_scope("z_wait"):
        send_z.wait_recv()
    with jax.named_scope("units_mate"):
        [units(i, 1) for i in range(2)]
    with jax.named_scope("wout_wait"):
        arrived(1)

    def project(t, write):
        def wide(q):
            write(pl.ds(pl.multiple_of(q * 384, 128), 256), dot(act[t], w_wide[1, q].reshape(D, 256)))

        def slim(i):
            w = jnp.concatenate([w_slim[1, 2 * i + n].reshape(D, 128) for n in range(2)], axis=1)
            res = dot(act[t], w)
            for n in range(2):
                write(pl.ds(pl.multiple_of((2 * i + n) * 384 + 256, 128), 128), res[:, n * 128 : (n + 1) * 128])

        loop(2, slim)
        loop(4, wide)

    def write_part(at, v):
        part[:, at] = v.astype(BF16)

    def write_own(at, v):
        own_t[:, at] = v

    with jax.named_scope("project_mate"):
        project(1, write_part)
    send_part = remote(part, precv, ps, pr, mate)
    send_part.start()

    with jax.named_scope("project_own"):
        project(0, write_own)
    with jax.named_scope("part_wait"):
        send_part.wait_recv()

    def finish(i):
        at = pl.ds(pl.multiple_of(i * 128, 128), 128)
        total = (own_t[:, at] + precv[:, at].astype(F32)).T
        shift = column(b_out, i)
        for to in (slice(0, 128), slice(128, 256)):
            out[at, to] = (hid[at, to] + total[:, to] + shift).astype(BF16)

    with jax.named_scope("finish"):
        loop(12, finish)

    loop(15, lambda i: to_block(15 - i).wait_send())
    loop(15, lambda i: to_plane(15 - i).wait_send())
    send_z.wait_send()
    send_part.wait_send()
    def sent(ph):
        for k in range(4):
            if k:
                z_move(ph, k, 0, False).wait_send()
                z_move(ph, k, 1, False).wait_send()
                ay(ph, k, False).wait_send()
                for way in range(3):
                    x_move(ph, k, way, False).wait_send()
            for way in range(2):
                y_move(ph, k, way, False).wait_send()
                ax(ph, k, way, False).wait_send()
            y_pass(ph, k, False).wait_send()
            ax_pass(ph, k, False).wait_send()

    with jax.named_scope("sent"):
        sent(0)
        sent(1)


def on_device(
    fields, norm1_gain, norm1_shift, spec_w1, spec_b1, spec_w2, spec_b2,
    norm2_gain, norm2_shift, w_in, b_in, w_out, b_out,
):
    forward, inverse = plane_tables()
    gain1, shift1, gain2, shift2, last = (
        v.reshape(12, 128) for v in (norm1_gain, norm1_shift, norm2_gain, norm2_shift, b_out)
    )
    vmem = pl.BlockSpec(memory_space=pltpu.VMEM)
    dma = pltpu.SemaphoreType.DMA
    res = pl.pallas_call(
        kernel,
        out_shape=jax.ShapeDtypeStruct((D, TOK), BF16),
        in_specs=[vmem] * 7 + [pl.BlockSpec(memory_space=pl.ANY)] * 2 + [vmem] * 6,
        out_specs=vmem,
        scratch_shapes=[
            pltpu.VMEM((D, TOK), BF16),
            pltpu.VMEM((16, 128, TOK), BF16),
            pltpu.VMEM((8, 2 * MODES, 256), F32),
            pltpu.VMEM((8, 2 * MODES, 256), BF16),
            pltpu.VMEM((16, 2 * CH, 256), F32),
            pltpu.VMEM((16, CH, TOK), BF16),
            pltpu.VMEM((D, TOK), BF16),
            pltpu.VMEM((D, TOK), F32),
            pltpu.VMEM((2, TOK, D), BF16),
            pltpu.VMEM((2, TOK, D), BF16),
            pltpu.VMEM((TOK, D), BF16),
            pltpu.VMEM((TOK, D), BF16),
            pltpu.VMEM((TOK, D), F32),
            pltpu.VMEM((2, 4, 16, CH, 256), BF16),
            pltpu.VMEM((2, 4, 16, CH, 128), BF16),
            pltpu.VMEM((2, 128, 128), F32),
            pltpu.VMEM((16, 128), F32),
            pltpu.VMEM((256, 256), BF16),
            pltpu.VMEM((2 * CH, 256), BF16),
            pltpu.VMEM((1, 256), F32),
            pltpu.VMEM((2 * CH, MODES), F32),
            pltpu.VMEM((4, 8, 384), F32),
            pltpu.VMEM((2 * MODES, TOK), BF16),
            pltpu.VMEM((512, TOK), BF16),
            dma((16,)), dma((16,)), dma((16,)), dma((16,)), dma((2, 6)),
            dma, dma, dma, dma,
            dma((2, 2, 4)), dma((2, 2, 4)), dma((2, 3, 4)), dma((2, 3, 4)), dma((2, 2, 4)), dma((2, 2, 4)),
            dma((2, 4)), dma((2, 4)), dma((2, 4)), dma((2, 4)), dma((2, 2, 4)), dma((2, 2, 4)),
            dma((2, 4)), dma((2, 4)),
        ],
        compiler_params=pltpu.CompilerParams(
            collective_id=0, has_side_effects=True, vmem_limit_bytes=56 * 2**20
        ),
        name="block",
    )(
        fields[0], gain1, shift1, gain2, shift2, last, b_in.reshape(24, 128), w_in.T, w_out,
        spec_w1, spec_b1, spec_w2, spec_b2, forward, inverse,
    )
    return res[None]


def solution(mesh):
    return jax.shard_map(
        on_device,
        mesh=mesh,
        in_specs=(
            P("batch", None, "chan"),
            P(),
            P(),
            P(None, "chan", None, None),
            P(None, "chan", None),
            P(None, "chan", None, None),
            P(None, "chan", None),
            P(),
            P(),
            P(None, "batch"),
            P(),
            P("batch", None),
            P(),
        ),
        out_specs=P("batch", None, "chan"),
        check_vma=False,
    )
```

```python
import math

import jax
import jax.numpy as jnp
import numpy as np
from jax import lax
from jax.experimental import pallas as pl
from jax.experimental.pallas import tpu as pltpu
from jax.sharding import PartitionSpec as P

D = 1536
TOK = 256
CH = 96
HALF = 48
GRID = 16
MODES = 144
SHRINK = 0.2
MESH = pl.DeviceIdType.MESH
F32 = jnp.float32
BF16 = jnp.bfloat16


def plane_tables():
    pos = np.arange(GRID)
    freq = np.arange(GRID // 2 + 1)
    phase = (
        pos[:, None, None, None] * pos[None, None, :, None]
        + pos[None, :, None, None] * freq[None, None, None, :]
    ) % GRID
    angle = phase * (2.0 * math.pi / GRID)
    cos = np.cos(angle).reshape(TOK, MODES) / 64.0
    sin = np.sin(angle).reshape(TOK, MODES) / 64.0
    weight = np.tile(np.where((freq == 0) | (freq == GRID // 2), 1.0, 2.0), GRID)
    forward = np.concatenate([cos, -sin], axis=1).T
    inverse = np.zeros((512, TOK))
    inverse[:MODES] = (cos * weight).T
    inverse[256 : 256 + MODES] = -(sin * weight).T
    return jnp.asarray(forward, F32), jnp.asarray(inverse, F32)


def turned(value, step, sign):
    re, im = value
    step = step % 16
    if step == 0:
        return value
    if step == 8:
        return (-re, -im)
    if step == 4:
        return (-im, re) if sign > 0 else (im, -re)
    if step == 12:
        return (im, -re) if sign > 0 else (-im, re)
    c = math.cos(2.0 * math.pi * step / 16)
    s = sign * math.sin(2.0 * math.pi * step / 16)
    return (re * c - im * s, re * s + im * c)


def fft_list(values, sign):
    n = len(values)
    if n == 1:
        return values
    even = fft_list(values[0::2], sign)
    odd = fft_list(values[1::2], sign)
    out = [None] * n
    for k in range(n // 2):
        t = turned(odd[k], k * (16 // n), sign)
        e = even[k]
        out[k] = (e[0] + t[0], e[1] + t[1])
        out[k + n // 2] = (e[0] - t[0], e[1] - t[1])
    return out


def gelu(v):
    size = jnp.abs(v)
    d = 1.0 + (0.3275911 * 0.7071067811865476) * size
    t = pl.reciprocal(d, approx=True)
    t = t * (2.0 - d * t)
    e = jnp.exp2(v * v * (-0.5 * 1.4426950408889634))
    q = 0.5 * 1.061405429 * t - 0.5 * 1.453152027
    q = q * t + 0.5 * 1.421413741
    q = q * t - 0.5 * 0.284496736
    q = q * t + 0.5 * 0.254829592
    return jnp.maximum(v, 0.0) - (q * t) * (e * size)


def shrink(v):
    return v - jnp.clip(v, -SHRINK, SHRINK)


class Several:
    def __init__(self, copies):
        self.copies = copies

    def start(self):
        for copy in self.copies:
            copy.start()

    def wait_recv(self):
        for copy in self.copies:
            copy.wait_recv()

    def wait_send(self):
        for copy in self.copies:
            copy.wait_send()


def dot_nt(a, b):
    return lax.dot_general(a, b, (((1,), (1,)), ((), ())), preferred_element_type=F32)


def dot(a, b):
    return jnp.dot(a, b, preferred_element_type=F32)


def loop(n, body, unroll=1, start=0):
    def step(i, carry):
        body(i)
        return carry

    lax.fori_loop(start, n, step, 0, unroll=unroll)


def kernel(
    fields, gain1, shift1, gain2, shift2, b_out, b_in, win, wout, w1, b1, w2, b2, fwd_table, inv_table, out,
    normed, recv1, plane, mid, back, fil, recv2, hid, zt, act, part, precv, own_t,
    w_wide, w_slim, tile, row, mix1, mix2, bias1, bias2, units_bias, fwd, inv,
    s1, r1, s2, r2, loc, zs, zr, ps, pr,
    zws, zwr, xs, xr, ys, yr, y2s, y2r, ays, ayr, axs, axr, ax2s, ax2r, aos, aor, aps, apr,
):
    chan = lax.axis_index("chan")
    batch = lax.axis_index("batch")
    x, zh, core = chan // 4, (chan // 2) % 2, chan % 2
    y, zl = batch // 4, batch % 4
    z = zh * 4 + zl

    def dev(xx, yy, zz, cc):
        xx, yy, zz = xx % 4, yy % 4, zz % 8
        return ((xx * 2 + zz // 4) * 2 + cc, yy * 4 + zz % 4)

    def remote(src, dst, ss, rs, to):
        return pltpu.make_async_remote_copy(
            src_ref=src, dst_ref=dst, send_sem=ss, recv_sem=rs, device_id=to, device_id_type=MESH
        )

    def peer(j, way):
        dz, dx, dc = j // 8, (j // 2) % 4, j % 2
        px, pz, pc = (x + way * dx + 4) % 4, (zh + dz) % 2, (core + dc) % 2
        return (px * 2 + pz) * 2 + pc

    zp, zm = dev(x, y, z + 1, core), dev(x, y, z + 7, core)
    zp2, zm2 = dev(x, y, z + 2, core), dev(x, y, z + 6, core)
    yp, ym, y2 = dev(x, y + 1, z, core), dev(x, y + 3, z, core), dev(x, y + 2, z, core)
    xp, xm, x2 = dev(x + 1, y, z, core), dev(x + 3, y, z, core), dev(x + 2, y, z, core)
    mate = dev(x, y, z, 1 - core)

    barrier = pltpu.get_barrier_semaphore()

    def greet(j, carry):
        pl.semaphore_signal(barrier, inc=1, device_id=(peer(j, 1), batch), device_id_type=MESH)
        return carry

    lax.fori_loop(1, 16, greet, 0)
    for to in (zp, zm, zp2, zm2, yp, ym, y2):
        pl.semaphore_signal(barrier, inc=1, device_id=to, device_id_type=MESH)

    offs = (0, 3, 1, 2)

    def slot(dy, k):
        return ((y + dy) % 4) * 4 + (zl + offs[k]) % 4

    own_slot = slot(0, 0)
    mine = pl.ds(pl.multiple_of(core * CH, CH), CH)
    keeps = []
    for ph, src in enumerate((win, wout)):
        for q in range(4):
            keeps.append(
                pltpu.make_async_copy(src.at[mine, pl.ds(384 * q, 256)], w_wide.at[ph, q, own_slot], loc.at[ph, q])
            )
            keeps.append(
                pltpu.make_async_copy(
                    src.at[mine, pl.ds(384 * q + 256, 128)], w_slim.at[ph, q, own_slot], loc.at[ph, 4 + q]
                )
            )
    for copy in keeps:
        copy.start()

    def rows(i):
        return pl.ds(pl.multiple_of(i * CH, CH), CH)

    def chunk(i):
        return pl.ds(pl.multiple_of(i * 128, 128), 128)

    def column(vec, i):
        return jnp.broadcast_to(vec[pl.ds(i, 1), :], (128, 128)).T

    def norm(load, gains, shifts, write, total=None):
        def add(i, acc):
            return acc + jnp.sum(load(i).reshape(16, 8, TOK), axis=0)

        if total is None:
            total = lax.fori_loop(0, 12, add, jnp.zeros((8, TOK), F32))
        mean = jnp.sum(total, axis=0, keepdims=True) * (1.0 / D)

        def add_square(i, acc):
            c = load(i) - mean
            return acc + jnp.sum((c * c).reshape(16, 8, TOK), axis=0)

        total = lax.fori_loop(0, 12, add_square, jnp.zeros((8, TOK), F32))
        var = jnp.sum(total, axis=0, keepdims=True) * (1.0 / D)
        scale = lax.rsqrt(var + 1e-05)

        def finish(i):
            c = (load(i) - mean) * scale
            gain, shift = column(gains, i), column(shifts, i)
            for at in (slice(0, 128), slice(128, 256)):
                write(i, at, (c[:, at] * gain + shift).astype(BF16))

        loop(12, finish)

    def load_fields(i):
        return fields[chunk(i), :].astype(F32)

    def write_normed(i, at, v):
        normed[chunk(i), at] = v

    norm(load_fields, gain1, shift1, write_normed)
    pl.semaphore_wait(barrier, 22)

    def to_block(j):
        return remote(
            normed.at[rows(peer(j, 1))], recv1.at[chan, pl.ds(0, CH)], s1.at[j], r1.at[j], (peer(j, 1), batch)
        )

    def from_plane(j):
        return remote(
            normed.at[rows(chan)], recv1.at[peer(j, -1), pl.ds(0, CH)], s1.at[j], r1.at[j], (peer(j, 1), batch)
        )

    def z_move(ph, k, wide, came):
        ref = w_wide if wide else w_slim
        at = ref.at[ph, x, slot(0, k if came else 0)]
        to = {1: zp, 2: zm, 3: dev(x, y, z + 2 + 4 * core, core)}[k]
        return remote(at, at, zws.at[ph, wide, k], zwr.at[ph, wide, k], to)

    def x_move(ph, k, way, came):
        at = w_wide.at[ph, (x + ((3, 1, 2)[way] if came else 0)) % 4, slot(0, k)]
        return remote(at, at, xs.at[ph, way, k], xr.at[ph, way, k], (xp, xm, x2)[way])

    def y_move(ph, k, way, came):
        at = w_wide.at[ph, :, slot((3, 1)[way] if came else 0, k)]
        return remote(at, at, ys.at[ph, way, k], yr.at[ph, way, k], (yp, ym)[way])

    def y_pass(ph, k, came):
        at = w_wide.at[ph, :, slot(2 if came else (3 if k < 2 else 1), k)]
        return remote(at, at, y2s.at[ph, k], y2r.at[ph, k], yp if k < 2 else ym)

    def group(ph, q, dy):
        return w_slim.at[ph, q, pl.ds(((y + dy) % 4) * 4, 4)]

    def ay(ph, r, came):
        at = group(ph, x, offs[r] if came else 0)
        return remote(at, at, ays.at[ph, r], ayr.at[ph, r], {1: yp, 2: ym, 3: y2}[r])

    def ax(ph, r, way, came):
        q = (x + ((3, 1)[way] if came else 0)) % 4
        if r == 0:
            parts = [(k, w_slim.at[ph, q, slot(0, k)]) for k in (1, 2, 3)]
            return Several(
                [remote(at, at, aos.at[ph, way, k], aor.at[ph, way, k], (xp, xm)[way]) for k, at in parts]
            )
        at = group(ph, q, offs[r])
        return remote(at, at, axs.at[ph, way, r], axr.at[ph, way, r], (xp, xm)[way])

    def ax_pass(ph, r, came):
        q = (x + (2 if came else (3 if r < 2 else 1))) % 4
        if r == 0:
            parts = [(k, w_slim.at[ph, q, slot(0, k)]) for k in (1, 2, 3)]
            return Several([remote(at, at, aps.at[ph, k], apr.at[ph, k], xp) for k, at in parts])
        at = group(ph, q, offs[r])
        return remote(at, at, ax2s.at[ph, r], ax2r.at[ph, r], xp if r < 2 else xm)

    def start_z(ph):
        for k in (1, 2, 3):
            z_move(ph, k, 1, False).start()
            z_move(ph, k, 0, False).start()

    def start_y(ph, k):
        y_move(ph, k, 0, False).start()
        y_move(ph, k, 1, False).start()

    for copy in keeps:
        copy.wait()
    start_z(0)
    start_z(1)
    loop(8, lambda i: to_block(15 - i).start())
    keep = pltpu.make_async_copy(normed.at[rows(chan)], recv1.at[chan, pl.ds(0, CH)], loc.at[0, 8])
    keep.start()

    start_y(0, 0)
    start_y(1, 0)
    loop(7, lambda i: to_block(7 - i).start())

    def service_z(ph):
        for k in (1, 2, 3):
            z_move(ph, k, 1, True).wait_recv()
            for way in range(3):
                x_move(ph, k, way, False).start()
            z_move(ph, k, 0, True).wait_recv()
        for r in (1, 2, 3):
            ay(ph, r, False).start()
        ax(ph, 0, 0, False).start()
        ax(ph, 0, 1, False).start()

    def service_x(ph):
        for k in (1, 2, 3):
            for way in range(3):
                x_move(ph, k, way, True).wait_recv()
            start_y(ph, k)

    def service_a(ph):
        for r in (1, 2, 3):
            ay(ph, r, True).wait_recv()
            ax(ph, r, 0, False).start()
            ax(ph, r, 1, False).start()

    def service_y(ph, ks):
        for k in ks:
            y_move(ph, k, 0 if k < 2 else 1, True).wait_recv()
            y_pass(ph, k, False).start()

    def service_ax(ph):
        for r in range(4):
            ax(ph, r, 0 if r < 2 else 1, True).wait_recv()
            ax_pass(ph, r, False).start()

    service_z(0)
    service_y(0, (0,))
    service_z(1)
    tile[...] = jnp.zeros_like(tile)
    row[...] = jnp.zeros_like(row)

    def diagonal(w, ri):
        tile[0, pl.ds(0, HALF), pl.ds(0, HALF)] = w[ri, 0]
        tile[1, pl.ds(HALF, HALF), pl.ds(0, HALF)] = w[ri, 1]
        return tile[0] + pltpu.roll(tile[1], HALF, 1)

    def bias_row(b, ri):
        row[pl.ds(0, 1), pl.ds(0, HALF)] = b[ri, pl.ds(0, 1)]
        row[pl.ds(8, 1), pl.ds(0, HALF)] = b[ri, pl.ds(1, 1)]
        both = row[pl.ds(0, 8), :] + pltpu.roll(row[pl.ds(8, 8), :], HALF, 1)
        return both[0:1]

    low, high = pl.ds(0, 128), pl.ds(128, 128)
    re, im = diagonal(w1, 0), diagonal(w1, 1)
    mix1[low, low], mix1[low, high] = re.astype(BF16), im.astype(BF16)
    mix1[high, low], mix1[high, high] = (-im).astype(BF16), re.astype(BF16)
    re, im = diagonal(w2, 0).T[:CH], diagonal(w2, 1).T[:CH]
    mix2[pl.ds(0, CH), low], mix2[pl.ds(0, CH), high] = re.astype(BF16), (-im).astype(BF16)
    mix2[pl.ds(CH, CH), low], mix2[pl.ds(CH, CH), high] = im.astype(BF16), re.astype(BF16)
    for ri in range(2):
        bias1[:, pl.ds(128 * ri, 128)] = bias_row(b1, ri)
        down = jnp.broadcast_to(bias_row(b2, ri), (128, 128)).T[:CH]
        bias2[pl.ds(CH * ri, CH), low] = down
        bias2[pl.ds(CH * ri, CH), pl.ds(128, 16)] = down[:, :16]

    fwd[...] = fwd_table[...].astype(BF16)
    inv[...] = inv_table[...].astype(BF16)
    lane = lax.broadcasted_iota(jnp.int32, (1, 768), 1)
    for g in range(4):
        six = jnp.concatenate([b_in[pl.ds(6 * g + i, 1), :] for i in range(6)], axis=1)
        six = jnp.where(core == 0, six, pltpu.roll(six, 768 - CH, 1))
        half = six
        for k in (1, 2, 3):
            half = jnp.where(lane < CH * k, half, pltpu.roll(six, 768 - CH * k, 1))
        units_bias[g, pl.ds(0, 1), :] = half[:, :384]

    def clear(a):
        recv1[a, pl.ds(CH, 32), :] = jnp.zeros((32, TOK), BF16)
        back[a, :, pl.ds(128, 128)] = jnp.zeros((2 * CH, 128), F32)

    loop(16, clear)

    keep.wait()
    service_x(0)
    service_a(0)
    service_y(1, (0,))

    service_x(1)
    service_y(0, (1,))

    def planes(p):
        both = recv1[pl.ds(2 * p, 2)].reshape(256, TOK)
        plane[p] = dot_nt(fwd[...], both)

    def planes_in(i):
        from_plane(2 * i).wait_recv()
        from_plane(2 * i + 1).wait_recv()
        planes(peer(2 * i, -1) // 2)

    from_plane(1).wait_recv()
    planes(chan // 2)
    loop(8, planes_in, start=1)


    def lines(t):
        re_at = pl.ds(pl.multiple_of(t * 8, 8), 8)
        im_at = pl.ds(pl.multiple_of(MODES + t * 8, 8), 8)
        vals = []
        for a in range(16):
            lanes = pl.ds((a % 2) * 128, 128)
            vals.append((plane[a // 2, re_at, lanes], plane[a // 2, im_at, lanes]))
        for a, (re, im) in enumerate(fft_list(vals, -1)):
            lanes = pl.ds((a % 2) * 128, 128)
            plane[a // 2, re_at, lanes] = re
            plane[a // 2, im_at, lanes] = im

    loop(18, lines, unroll=2)

    def mix_in(p):
        v = plane[p].astype(BF16)
        lhs = jnp.concatenate(
            [
                jnp.concatenate([v[:MODES, :128], v[MODES:, :128]], axis=1),
                jnp.concatenate([v[:MODES, 128:], v[MODES:, 128:]], axis=1),
            ],
            axis=0,
        )
        mid[p] = gelu(dot(lhs, mix1[...]) + bias1[...]).astype(BF16)

    def mix_out(p):
        for half in range(2):
            res = dot_nt(mix2[...], mid[p, pl.ds(half * MODES, MODES), :]) + bias2[...]
            back[2 * p + half, :, pl.ds(0, MODES)] = shrink(res)

    loop(8, mix_in, unroll=2)
    loop(8, mix_out, unroll=2)
    service_y(0, (2, 3))
    service_a(1)

    def lines_back(t):
        re_at = pl.ds(pl.multiple_of((t // 2) * 8, 8), 8)
        im_at = pl.ds(pl.multiple_of(CH + (t // 2) * 8, 8), 8)
        lanes = pl.ds(pl.multiple_of((t % 2) * 128, 128), 128)
        vals = [(back[a, re_at, lanes], back[a, im_at, lanes]) for a in range(16)]
        for a, (re, im) in enumerate(fft_list(vals, 1)):
            back[a, re_at, lanes] = re
            back[a, im_at, lanes] = im

    loop(24, lines_back, unroll=2)

    def planes_back(p):
        lhs = [
            jnp.concatenate([back[2 * p + i, :CH, :], back[2 * p + i, CH:, :]], axis=1).astype(BF16)
            for i in range(2)
        ]
        res = dot(jnp.concatenate(lhs, axis=0), inv[...])
        for i in range(2):
            v = res[i * CH : (i + 1) * CH] + recv1[2 * p + i, pl.ds(0, CH), :].astype(F32)
            fil[2 * p + i] = v.astype(BF16)

    def to_plane(j):
        return remote(fil.at[peer(j, 1)], recv2.at[rows(chan)], s2.at[j], r2.at[j], (peer(j, 1), batch))

    def from_block(j):
        return remote(fil.at[chan], recv2.at[rows(peer(j, -1))], s2.at[j], r2.at[j], (peer(j, 1), batch))

    def planes_out(i):
        planes_back(peer(14 - 2 * i, 1) // 2)
        to_plane(14 - 2 * i).start()
        to_plane(15 - 2 * i).start()

    loop(7, planes_out)
    planes_back(chan // 2)
    to_plane(1).start()
    keep = pltpu.make_async_copy(fil.at[chan], recv2.at[rows(chan)], loc.at[1, 8])
    keep.start()
    service_y(1, (1,))
    service_ax(0)
    service_y(1, (2, 3))
    service_ax(1)
    keep.wait()

    def take(p, acc):
        v = fields[rows(p), :].astype(F32) + recv2[rows(p), :].astype(F32)
        hid[rows(p), :] = v
        return acc + jnp.sum(v.reshape(CH // 8, 8, TOK), axis=0)

    def take_next(j, acc):
        from_block(j).wait_recv()
        return take(peer(j, -1), acc)

    channel_sum = lax.fori_loop(1, 16, take_next, take(chan, jnp.zeros((8, TOK), F32)))

    def write_z(i, at, v):
        recv2[chunk(i), at] = v

    def load_hidden(i):
        return hid[chunk(i), :]

    norm(load_hidden, gain2, shift2, write_z, channel_sum)

    eye = (
        lax.broadcasted_iota(jnp.int32, (TOK, TOK), 0) == lax.broadcasted_iota(jnp.int32, (TOK, TOK), 1)
    ).astype(F32).astype(BF16)

    def turn(i):
        at = pl.ds(pl.multiple_of(i * 256, 256), 256)
        zt[0, :, at] = dot_nt(eye, recv2[at, :]).astype(BF16)

    loop(6, turn)
    send_z = remote(zt.at[0], zt.at[1], zs, zr, mate)
    send_z.start()

    def units(i, t):
        g = [(y + offs[2 * i + n]) % 4 for n in range(2)]

        def shards(n):
            at = pl.ds(g[n] * 4, 4)
            parts = [
                (w_wide[0, q, at].reshape(384, 256), w_slim[0, q, at].reshape(384, 128)) for q in range(4)
            ]
            return jnp.concatenate([v for pair in parts for v in pair], axis=1)

        res = dot_nt(zt[t], jnp.concatenate([shards(0), shards(1)], axis=0))
        for n in range(2):
            at = pl.ds(pl.multiple_of(g[n] * 384, 128), 384)
            act[t, :, at] = gelu(res[:, n * 384 : (n + 1) * 384] + units_bias[g[n], pl.ds(0, 1), :]).astype(BF16)

    def arrived(ph):
        for k in range(4):
            y_move(ph, k, 0 if k >= 2 else 1, True).wait_recv()
        for r in range(4):
            ax(ph, r, 0 if r >= 2 else 1, True).wait_recv()
        for k in range(4):
            ax_pass(ph, k, True).wait_recv()
        for k in range(4):
            y_pass(ph, k, True).wait_recv()

    for k in (2, 3):
        y_move(0, k, 0, True).wait_recv()
    for r in range(4):
        ax(0, r, 0 if r >= 2 else 1, True).wait_recv()
    for k in range(4):
        ax_pass(0, k, True).wait_recv()
    units(0, 0)
    for k in (0, 1):
        y_move(0, k, 1, True).wait_recv()
    for k in range(4):
        y_pass(0, k, True).wait_recv()
    units(1, 0)
    send_z.wait_recv()
    [units(i, 1) for i in range(2)]
    arrived(1)

    def project(t, write):
        def wide(q):
            write(pl.ds(pl.multiple_of(q * 384, 128), 256), dot(act[t], w_wide[1, q].reshape(D, 256)))

        def slim(i):
            w = jnp.concatenate([w_slim[1, 2 * i + n].reshape(D, 128) for n in range(2)], axis=1)
            res = dot(act[t], w)
            for n in range(2):
                write(pl.ds(pl.multiple_of((2 * i + n) * 384 + 256, 128), 128), res[:, n * 128 : (n + 1) * 128])

        loop(2, slim)
        loop(4, wide)

    def write_part(at, v):
        part[:, at] = v.astype(BF16)

    def write_own(at, v):
        own_t[:, at] = v

    project(1, write_part)
    send_part = remote(part, precv, ps, pr, mate)
    send_part.start()

    project(0, write_own)
    send_part.wait_recv()

    def finish(i):
        at = pl.ds(pl.multiple_of(i * 128, 128), 128)
        total = (own_t[:, at] + precv[:, at].astype(F32)).T
        shift = column(b_out, i)
        for to in (slice(0, 128), slice(128, 256)):
            out[at, to] = (hid[at, to] + total[:, to] + shift).astype(BF16)

    loop(12, finish)

    loop(15, lambda i: to_block(15 - i).wait_send())
    loop(15, lambda i: to_plane(15 - i).wait_send())
    send_z.wait_send()
    send_part.wait_send()
    def sent(ph):
        for k in range(4):
            if k:
                z_move(ph, k, 0, False).wait_send()
                z_move(ph, k, 1, False).wait_send()
                ay(ph, k, False).wait_send()
                for way in range(3):
                    x_move(ph, k, way, False).wait_send()
            for way in range(2):
                y_move(ph, k, way, False).wait_send()
                ax(ph, k, way, False).wait_send()
            y_pass(ph, k, False).wait_send()
            ax_pass(ph, k, False).wait_send()

    sent(0)
    sent(1)


def on_device(
    fields, norm1_gain, norm1_shift, spec_w1, spec_b1, spec_w2, spec_b2,
    norm2_gain, norm2_shift, w_in, b_in, w_out, b_out,
):
    forward, inverse = plane_tables()
    gain1, shift1, gain2, shift2, last = (
        v.reshape(12, 128) for v in (norm1_gain, norm1_shift, norm2_gain, norm2_shift, b_out)
    )
    vmem = pl.BlockSpec(memory_space=pltpu.VMEM)
    dma = pltpu.SemaphoreType.DMA
    res = pl.pallas_call(
        kernel,
        out_shape=jax.ShapeDtypeStruct((D, TOK), BF16),
        in_specs=[vmem] * 7 + [pl.BlockSpec(memory_space=pl.ANY)] * 2 + [vmem] * 6,
        out_specs=vmem,
        scratch_shapes=[
            pltpu.VMEM((D, TOK), BF16),
            pltpu.VMEM((16, 128, TOK), BF16),
            pltpu.VMEM((8, 2 * MODES, 256), F32),
            pltpu.VMEM((8, 2 * MODES, 256), BF16),
            pltpu.VMEM((16, 2 * CH, 256), F32),
            pltpu.VMEM((16, CH, TOK), BF16),
            pltpu.VMEM((D, TOK), BF16),
            pltpu.VMEM((D, TOK), F32),
            pltpu.VMEM((2, TOK, D), BF16),
            pltpu.VMEM((2, TOK, D), BF16),
            pltpu.VMEM((TOK, D), BF16),
            pltpu.VMEM((TOK, D), BF16),
            pltpu.VMEM((TOK, D), F32),
            pltpu.VMEM((2, 4, 16, CH, 256), BF16),
            pltpu.VMEM((2, 4, 16, CH, 128), BF16),
            pltpu.VMEM((2, 128, 128), F32),
            pltpu.VMEM((16, 128), F32),
            pltpu.VMEM((256, 256), BF16),
            pltpu.VMEM((2 * CH, 256), BF16),
            pltpu.VMEM((1, 256), F32),
            pltpu.VMEM((2 * CH, MODES), F32),
            pltpu.VMEM((4, 8, 384), F32),
            pltpu.VMEM((2 * MODES, TOK), BF16),
            pltpu.VMEM((512, TOK), BF16),
            dma((16,)), dma((16,)), dma((16,)), dma((16,)), dma((2, 9)),
            dma, dma, dma, dma,
            dma((2, 2, 4)), dma((2, 2, 4)), dma((2, 3, 4)), dma((2, 3, 4)), dma((2, 2, 4)), dma((2, 2, 4)),
            dma((2, 4)), dma((2, 4)), dma((2, 4)), dma((2, 4)), dma((2, 2, 4)), dma((2, 2, 4)),
            dma((2, 4)), dma((2, 4)), dma((2, 2, 4)), dma((2, 2, 4)), dma((2, 4)), dma((2, 4)),
        ],
        compiler_params=pltpu.CompilerParams(
            collective_id=0, has_side_effects=True, vmem_limit_bytes=56 * 2**20
        ),
        name="block",
    )(
        fields[0], gain1, shift1, gain2, shift2, last, b_in.reshape(24, 128), w_in.T, w_out,
        spec_w1, spec_b1, spec_w2, spec_b2, forward, inverse,
    )
    return res[None]


def solution(mesh):
    return jax.shard_map(
        on_device,
        mesh=mesh,
        in_specs=(
            P("batch", None, "chan"),
            P(),
            P(),
            P(None, "chan", None, None),
            P(None, "chan", None),
            P(None, "chan", None, None),
            P(None, "chan", None),
            P(),
            P(),
            P(None, "batch"),
            P(),
            P("batch", None),
            P(),
        ),
        out_specs=P("batch", None, "chan"),
        check_vma=False,
    )
```
